512 devices in a mesh: gx: 32 (over y, x), gy: 16 (over z, core).
Axes of the slice: x: 4, y: 8, z: 8, core: 2. Of those that a mesh axis runs over, the one named last changes fastest.
Arguments:
- right_sides: bfloat16 [32, 16, 512, 144], P('gx', 'gy'), may hold values from -6 to 6
- near_self: bfloat16 [32, 16, 512, 512], P('gx', 'gy'), may hold values from -0.09375 to 0.09375
- near_blocks: bfloat16 [32, 16, 4, 512, 512], P('gx', 'gy'), may hold values from -0.09375 to 0.09375
- near_list: int32 [32, 16, 4], P('gx', 'gy'), may hold values from -1 to 511, as said below
- basis: bfloat16 [32, 16, 512, 160], P('gx', 'gy'), may hold values from -0.25 to 0.25
- transfer_one: bfloat16 [32, 16, 160, 160], P('gx', 'gy'), may hold values from -0.25 to 0.25
- transfer_two: bfloat16 [32, 16, 40, 160], P('gx', 'gy'), may hold values from -0.3125 to 0.3125
- couple_one: bfloat16 [32, 16, 7, 160, 160], P('gx', 'gy'), may hold values from -0.09375 to 0.09375
- couple_two: bfloat16 [32, 16, 4, 160, 160], P('gx', 'gy'), may hold values from -0.09375 to 0.09375
- far_list_one: int32 [32, 16, 7], P('gx', 'gy'), may hold values from -1 to 127, as said below
- far_list_two: int32 [32, 16, 4], P('gx', 'gy'), may hold values from -1 to 63, as said below
Outputs:
- applied: bfloat16 [32, 16, 512, 144], P('gx', 'gy')
The draws below stay inside these ranges and needn't reach their ends.
Inputs may be any that keep to these rules, and one draw needn't show every extreme that they name: `near_list`: the four entries of leaf (i, j) name, in some order, the leaves (i, j + 1), (i + 1, j - 1), (i + 1, j), (i + 1, j + 1), each once, or -1 where that leaf lies outside the grid of 32 x 16 leaves. `far_list_one`: each entry is -1 or the index of a first-level cluster (c, d) with c - a in -2 - a % 2 to 3 - a % 2 and d - b in -2 - b % 2 to 3 - b % 2 that is not adjacent to the leaf's own first-level cluster (a, b); over the four leaves of a first-level cluster every such cluster inside the grid is named exactly once. `far_list_two`: each entry is -1 or the index of a second-level cluster (c, d) with c - a in -2 - a % 2 to 3 - a % 2 and d - b in -2 - b % 2 to 3 - b % 2 that is not adjacent to the leaf's own second-level cluster (a, b); over the eight leaves of a second-level cluster every such cluster inside the grid is named exactly once.
All inputs are finite; a program needn't handle non-finite values.
Results may differ from the reference program's by a relative error of at most 0.012.
Values may be sent and summed in bfloat16 or wider, within the bound.
No kernel may reach another device: no remote copies, remote signals or barrier semaphores. Data moves between devices by JAX's collectives and lax.ppermute only.
A program may use at most 64 MiB of HBM per device.

```python
import jax
import jax.numpy as jnp
import numpy as np

LEAF = 512
RANK = 160
NRHS = 144
SLOTS_ONE = 7
SLOTS_TWO = 4
GX = 32
GY = 16


def offset_table():
    offsets = np.zeros((2, 2, 27, 2), np.int32)
    for row_parity in range(2):
        for col_parity in range(2):
            counter = 0
            for down_off in range(-2 - row_parity, 4 - row_parity):
                for side_off in range(-2 - col_parity, 4 - col_parity):
                    if abs(down_off) > 1 or abs(side_off) > 1:
                        offsets[row_parity, col_parity, counter, 0] = down_off
                        offsets[row_parity, col_parity, counter, 1] = side_off
                        counter += 1
    return offsets


def far_links(key, row_stride, col_stride, slots):
    level_rows = GX // row_stride
    level_cols = GY // col_stride
    rotation = jax.random.randint(key, (level_rows, level_cols), 0, 27)
    offsets = jnp.asarray(offset_table())
    device_row = jnp.arange(GX, dtype=jnp.int32)[:, None, None]
    device_col = jnp.arange(GY, dtype=jnp.int32)[None, :, None]
    slot_index = jnp.arange(slots, dtype=jnp.int32)[None, None, :]
    cluster_row = device_row // row_stride
    cluster_col = device_col // col_stride
    members = row_stride * col_stride
    position = device_row % row_stride * col_stride + device_col % col_stride
    serial = slot_index * members + position
    chosen = (serial + rotation[cluster_row, cluster_col]) % 27
    picked = offsets[cluster_row % 2, cluster_col % 2, chosen]
    source_row = cluster_row + picked[..., 0]
    source_col = cluster_col + picked[..., 1]
    inside = (serial < 27) & (source_row >= 0) & (source_row < level_rows) & (source_col >= 0) & (source_col < level_cols)
    return jnp.where(inside, source_row * level_cols + source_col, -1).astype(jnp.int32)


def draw_near_list(key, part):
    key = jax.random.fold_in(key, 11)
    rotation = jax.random.randint(key, (GX, GY, 1), 0, 4)
    down_steps = jnp.array([0, 1, 1, 1], dtype=jnp.int32)
    side_steps = jnp.array([1, -1, 0, 1], dtype=jnp.int32)
    chosen = (jnp.arange(4, dtype=jnp.int32)[None, None, :] + rotation) % 4
    source_row = jnp.arange(GX, dtype=jnp.int32)[:, None, None] + down_steps[chosen]
    source_col = jnp.arange(GY, dtype=jnp.int32)[None, :, None] + side_steps[chosen]
    inside = (source_row < GX) & (source_col >= 0) & (source_col < GY)
    return jnp.where(inside, source_row * GY + source_col, -1).astype(jnp.int32)


def draw_far_list_one(key, part):
    key = jax.random.fold_in(key, 12)
    return far_links(key, 2, 2, SLOTS_ONE)


def draw_far_list_two(key, part):
    key = jax.random.fold_in(key, 13)
    return far_links(key, 2, 4, SLOTS_TWO)


def block_scale(stream_key, shape, cuts, low, top_value):
    def one(axis_at, blocks):
        heights = jax.random.uniform(jax.random.fold_in(jax.random.fold_in(stream_key, 6), axis_at), (blocks,), jnp.float32, low / len(cuts), top_value / len(cuts))
        return jnp.repeat(jnp.exp(heights), shape[axis_at] // blocks).reshape((-1,) + (1,) * (len(shape) - axis_at - 1))

    level = one(*cuts[0])
    for cut in cuts[1:]:
        level = level * one(*cut)
    return level


def centred(rng, extent, scale, bound, shards=(), held_as=jnp.bfloat16):
    entries = jax.random.normal(rng, extent, jnp.float32) * scale
    if len(shards) > 0:
        entries = block_scale(rng, extent, shards, -0.22, 0.18) * entries
    return jnp.clip(entries, min=-bound, max=bound).astype(held_as)


def setup_inputs(seed: int = 0) -> dict:
    arg_keys = jax.random.split(jax.random.key(seed), 12)
    right_sides = centred(arg_keys[0], (GX, GY, LEAF, NRHS), 1.0, 6.0, ((0, 32), (1, 16)))
    near_self = centred(arg_keys[1], (GX, GY, LEAF, LEAF), (9 * LEAF) ** -0.5, 0.09375, ((0, 32), (1, 16)))
    near_blocks = centred(arg_keys[2], (GX, GY, 4, LEAF, LEAF), (9 * LEAF) ** -0.5, 0.09375, ((0, 32), (1, 16)))
    near_list = draw_near_list(jax.random.fold_in(arg_keys[11], 71), 0)
    basis = centred(arg_keys[4], (GX, GY, LEAF, RANK), LEAF ** -0.5, 0.25, ((0, 32), (1, 16)))
    transfer_one = centred(arg_keys[5], (GX, GY, RANK, RANK), (4 * RANK) ** -0.5, 0.25, ((0, 32), (1, 16)))
    transfer_two = centred(arg_keys[6], (GX, GY, RANK // 4, RANK), (2 * RANK) ** -0.5, 0.3125, ((0, 32), (1, 16)))
    couple_one = centred(arg_keys[7], (GX, GY, SLOTS_ONE, RANK, RANK), (27 * RANK) ** -0.5, 0.09375, ((0, 32), (1, 16)))
    couple_two = centred(arg_keys[8], (GX, GY, SLOTS_TWO, RANK, RANK), (27 * RANK) ** -0.5, 0.09375, ((0, 32), (1, 16)))
    far_list_one = draw_far_list_one(jax.random.fold_in(arg_keys[11], 71), 0)
    far_list_two = draw_far_list_two(jax.random.fold_in(arg_keys[11], 71), 0)
    return {"right_sides": right_sides, "near_self": near_self, "near_blocks": near_blocks, "near_list": near_list, "basis": basis, "transfer_one": transfer_one, "transfer_two": transfer_two, "couple_one": couple_one, "couple_two": couple_two, "far_list_one": far_list_one, "far_list_two": far_list_two}


def widen(values):
    return values.astype(jnp.float32)


def block_sum(values, row_stride, col_stride):
    array_shape = values.shape
    grouped = values.reshape((array_shape[0] // row_stride, row_stride, array_shape[1] // col_stride, col_stride) + array_shape[2:])
    return jnp.sum(grouped, axis=(1, 3))


def spread(values, row_stride, col_stride):
    return jnp.repeat(jnp.repeat(values, row_stride, axis=0), col_stride, axis=1)


def far_terms(coefficients, couplings, sources):
    flat_coeff = coefficients.reshape((-1,) + coefficients.shape[2:])
    is_valid = sources >= 0
    selected = widen(flat_coeff[jnp.maximum(sources, 0)])
    selected = jnp.where(is_valid[..., None, None], selected, 0.0)
    return jnp.einsum("ijkrs,ijksn->ijrn", widen(couplings), selected)


def reference(right_sides, near_self, near_blocks, near_list, basis, transfer_one, transfer_two, couple_one, couple_two, far_list_one, far_list_two):
    leaves = GX * GY
    flat_x = right_sides.reshape(leaves, LEAF, NRHS)
    wide_x = widen(flat_x)
    near_sum = jnp.einsum("lab,lbn->lan", widen(near_self.reshape(leaves, LEAF, LEAF)), wide_x)
    leaf_links = near_list.reshape(leaves, 4)
    stored_blocks = near_blocks.reshape(leaves, 4, LEAF, LEAF)
    for slot_index in range(4):
        source = leaf_links[:, slot_index]
        is_valid = (source >= 0)[:, None, None]
        safe_source = jnp.maximum(source, 0)
        near_block = widen(stored_blocks[:, slot_index])
        direct = jnp.einsum("lab,lbn->lan", near_block, wide_x[safe_source])
        near_sum = near_sum + jnp.where(is_valid, direct, 0.0)
        mirror = jnp.einsum("lba,lbn->lan", near_block, wide_x).astype(jnp.bfloat16)
        near_sum = near_sum.at[safe_source].add(jnp.where(is_valid, widen(mirror), 0.0))
    leaf_coeff = jnp.einsum("ijar,ijan->ijrn", widen(basis), widen(right_sides)).astype(jnp.bfloat16)
    up_one = jnp.einsum("ijrs,ijrn->ijsn", widen(transfer_one), widen(leaf_coeff))
    coeff_one = block_sum(up_one, 2, 2).astype(jnp.bfloat16)
    pieces = transfer_two.reshape(GX // 2, 2, GY // 2, 2, RANK // 4, RANK)
    level_two = pieces.transpose(0, 2, 1, 3, 4, 5).reshape(GX // 2, GY // 2, RANK, RANK)
    up_two = jnp.einsum("ijrs,ijrn->ijsn", widen(level_two), widen(coeff_one))
    coeff_two = block_sum(up_two, 1, 2).astype(jnp.bfloat16)
    local_two = block_sum(far_terms(coeff_two, couple_two, far_list_two), 2, 4).astype(jnp.bfloat16)
    down_two = jnp.einsum("ijrs,ijsn->ijrn", widen(level_two), widen(spread(local_two, 1, 2)))
    local_one = (block_sum(far_terms(coeff_one, couple_one, far_list_one), 2, 2) + down_two).astype(jnp.bfloat16)
    leaf_local = jnp.einsum("ijrs,ijsn->ijrn", widen(transfer_one), widen(spread(local_one, 2, 2))).astype(jnp.bfloat16)
    far_field = jnp.einsum("ijar,ijrn->ijan", widen(basis), widen(leaf_local))
    return (near_sum.reshape(GX, GY, LEAF, NRHS) + far_field).astype(jnp.bfloat16)
```

```python
import functools

import jax
import jax.numpy as jnp
from jax import lax
from jax.experimental import pallas as pl
from jax.experimental.pallas import tpu as pltpu
from jax.sharding import Mesh, PartitionSpec as P

AXES = ("y", "xh", "xl", "zh", "zl", "c")
F32, BF16, I32 = jnp.float32, jnp.bfloat16, jnp.int32
RANK, CHUNK, PAD = 160, 36, 40
SLOTS = (7, 4)
VMEM = pl.BlockSpec(memory_space=pltpu.VMEM)
SMEM = pl.BlockSpec(memory_space=pltpu.SMEM)


def call(body, outs, scratch, specs, flops, moved):
    return pl.pallas_call(
        body,
        out_shape=outs,
        in_specs=specs,
        out_specs=jax.tree.map(lambda _: VMEM, outs),
        scratch_shapes=scratch,
        compiler_params=pltpu.CompilerParams(vmem_limit_bytes=24 * 2**20),
        cost_estimate=pl.CostEstimate(flops=flops, bytes_accessed=moved, transcendentals=0),
    )


def shape(*dims, dtype=BF16):
    return jax.ShapeDtypeStruct(dims, dtype)


def mul(a, b):
    return lax.dot_general(a, b, (((1,), (0,)), ((), ())), preferred_element_type=F32)


def mul_t(a, b):
    return lax.dot_general(a, b, (((1,), (1,)), ((), ())), preferred_element_type=F32)


def spreader(groups, cols, transposed=False):
    dims = (cols, groups * PAD) if transposed else (groups * PAD, cols)
    padded = lax.broadcasted_iota(I32, dims, 1 if transposed else 0)
    dense = lax.broadcasted_iota(I32, dims, 0 if transposed else 1)
    hit = jnp.zeros(dims, jnp.bool_)
    for g in range(groups):
        inside = (padded >= PAD * g) & (padded < PAD * g + CHUNK)
        hit = hit | (inside & (dense == padded - (PAD - CHUNK) * g))
    return jnp.where(hit, 1.0, 0.0).astype(BF16)


def packed(a, b, tail, wide):
    wide[0, :, :RANK] = a
    wide[1, :, :RANK] = b
    rest = wide[0, :, 128:] + pltpu.roll(wide[1, :, 128:], 32, 1)
    return jnp.concatenate([wide[0, :, :128], wide[1, :, :128], rest, tail], axis=0).astype(BF16)


def up_body(x_ref, basis_ref, one_ref, two_ref, far_one_ref, far_two_ref, out_ref, wide, tail):
    wide[...] = jnp.zeros_like(wide)
    tail[...] = jnp.zeros_like(tail)
    tail[0:1, : SLOTS[0]] = far_one_ref[...]
    tail[1:2, : SLOTS[1]] = far_two_ref[...]
    last = tail[...].astype(F32)
    leaf = mul_t(x_ref[...], basis_ref[...]).astype(BF16)
    up = mul(leaf, one_ref[...]).astype(BF16)
    chunks = mul(spreader(4, 144), up)
    quarter = two_ref[...].astype(F32)
    for q in range(4):
        block = packed(chunks[PAD * q : PAD * (q + 1)], quarter, last, wide)
        for xh in range(2):
            for zl in range(2):
                out_ref[xh * 8 + (q // 2) * 4 + zl * 2 + q % 2] = block


def merge_body(me_ref, got_ref, window_ref, level_ref, lists_ref, wide, levels):
    me = me_ref[0]
    own = (me // 32) % 2 * 2 + me // 2 % 2
    groups = []
    for xh in range(2):
        second = jnp.zeros((PAD, RANK), F32)
        for zl in range(2):
            main = jnp.zeros((PAD, 128), F32)
            rest = jnp.zeros((PAD, 128), F32)
            for q in range(4):
                block = got_ref[xh * 8 + (q // 2) * 4 + zl * 2 + q % 2].astype(F32)
                main += block[:PAD]
                rest += block[2 * PAD : 3 * PAD]
                rows = slice(PAD * q, PAD * (q + 1))
                levels[xh * 2 + zl, rows, :128] = block[PAD : 2 * PAD]
                levels[xh * 2 + zl, rows, 128:] = pltpu.roll(block[2 * PAD : 3 * PAD], 96, 1)
            wide[:, :128] = main
            wide[:, 128:] = rest
            first = wide[:, :RANK]
            groups.append(first)
            second += mul(first.astype(BF16), levels[xh * 2 + zl, :, :RANK].astype(BF16))
        groups.append(second)
    stack = jnp.concatenate(groups, axis=0).astype(BF16)
    window_ref[...] = lax.dot_general(
        stack, spreader(6, 256), (((0,), (0,)), ((), ())), preferred_element_type=F32
    ).astype(BF16)
    level_ref[...] = levels[own, :, :RANK].astype(BF16)
    for q in range(4):
        place = (me // 32) % 2 * 8 + (q // 2) * 4 + me // 2 % 2 * 2 + q % 2
        tail = got_ref[place, 112:, :].astype(F32)
        lists_ref[q : q + 1, :] = tail[8:9].astype(I32)
        lists_ref[4 + q : 5 + q, :] = tail[9:10].astype(I32)


def pack_body(one_ref, two_ref, out_ref, wide):
    wide[...] = jnp.zeros_like(wide)
    for k in range(sum(SLOTS)):
        block = one_ref[k] if k < SLOTS[0] else two_ref[k - SLOTS[0]]
        out_ref[k, :RANK, :] = block[:, :128]
        wide[:, :32] = block[:, 128:].astype(F32)
        rest = wide[0:PAD]
        for r in range(1, 4):
            rest += pltpu.roll(wide[PAD * r : PAD * (r + 1)], 32 * r, 1)
        out_ref[k, RANK:, :] = rest.astype(BF16)


def couple_body(me_ref, lists_ref, up_ref, mid_ref, down_ref, own_ref, beside_ref, across_ref, out_ref, rows, total, matrix, wide):
    me = me_ref[0]
    y = me // 64
    q_own = me // 16 % 2 * 2 + me % 2
    rows[0] = up_ref[...]
    rows[1] = mid_ref[...]
    rows[2] = down_ref[...]
    total[...] = jnp.zeros_like(total)
    lane = lax.broadcasted_iota(I32, (RANK, 256), 1)
    slots = sum(SLOTS)

    def step(k, source, offset, q):
        second = k >= SLOTS[0]
        code = lists_ref[jnp.where(second, 4 + q, q), jnp.where(second, k - SLOTS[0], k)]
        valid = code >= 0
        safe = jnp.where(valid, code, y * jnp.where(second, 8, 16))
        width = jnp.where(second, 4, 8)
        row, col = safe // width, safe % width
        zh = jnp.where(second, col, col // 2)
        group = row % 2 * 3 + jnp.where(second, 2, col % 2)
        low = jnp.where(valid, group * CHUNK, 512)
        block = rows[row // 2 - y + 1, zh]
        block = jnp.where((lane >= low) & (lane < low + CHUNK), block.astype(F32), 0.0).astype(BF16)
        matrix[:, :128] = source[offset + k, :RANK, :].astype(F32)
        rest = source[offset + k, RANK:, :].astype(F32)
        for r in range(4):
            matrix[PAD * r : PAD * (r + 1), 128:] = rest if r == 0 else pltpu.roll(rest, 128 - 32 * r, 1)
        total[...] += mul(matrix[:, :RANK].astype(BF16), block)

    def every(k, carry):
        step(k, own_ref, 0, q_own)
        step(k, beside_ref, 0, q_own ^ 2)
        step(k, across_ref, 0, q_own ^ 1)
        step(k, across_ref, slots, q_own ^ 3)
        return carry

    lax.fori_loop(0, slots, every, 0)
    high = total[...].astype(BF16)
    low = (total[...] - high.astype(F32)).astype(BF16)
    r = lax.broadcasted_iota(I32, (PAD, 256), 0)
    c = lax.broadcasted_iota(I32, (PAD, 256), 1)
    results = []
    for members in ((0, 1, 3, 4), (2, 5)):
        hit = jnp.zeros((PAD, 256), jnp.bool_)
        for g in members:
            hit = hit | ((c == r + CHUNK * g) & (r < CHUNK))
        picker = jnp.where(hit, 1.0, 0.0).astype(BF16)
        results.append(mul_t(picker, high) + mul_t(picker, low))
    wide[...] = jnp.zeros_like(wide)
    block = packed(results[0], results[1], jnp.zeros((8, 128), F32), wide)
    for d in range(8):
        out_ref[d] = block


def down_body(me_ref, got_ref, level_ref, one_ref, basis_ref, near_ref, out_ref, wide, local):
    me = me_ref[0]
    zl_own = me // 2 % 2
    for q in range(4):
        base = q // 2 * 4 + q % 2
        mine = got_ref[base + zl_own * 2].astype(F32)
        both = got_ref[base].astype(F32) + got_ref[base + 2].astype(F32)
        wide[:, :128] = both[PAD : 2 * PAD]
        wide[:, 128:] = pltpu.roll(both[2 * PAD : 3 * PAD], 96, 1)
        second = wide[:, :RANK].astype(BF16)
        wide[:, :128] = mine[:PAD]
        wide[:, 128:] = mine[2 * PAD : 3 * PAD]
        local[PAD * q : PAD * (q + 1), :] = wide[:, :RANK] + mul_t(second, level_ref[...])
    one = mul(spreader(4, 144, True), local[...].astype(BF16)).astype(BF16)
    leaf = mul_t(one, one_ref[...]).astype(BF16)
    out_ref[...] = (near_ref[...] + mul(leaf, basis_ref[...])).astype(BF16)


def slot_of(list_ref, me, apart):
    found = jnp.int32(0)
    for k in range(1, 4):
        found = jnp.where(list_ref[0, k] == me + apart, k, found)
    return found


def mirror_body(me_ref, list_ref, x_ref, blocks_ref, left_ref, right_ref, below_ref):
    me = me_ref[0]
    x = x_ref[...]
    left_ref[0] = x
    right_ref[0] = x
    right_ref[1] = mul(x, blocks_ref[slot_of(list_ref, me, 1)]).astype(BF16)
    left_ref[1] = mul(x, blocks_ref[slot_of(list_ref, me, 15)]).astype(BF16)
    below_ref[...] = mul(x, blocks_ref[slot_of(list_ref, me, 16)]).astype(BF16)
    right_ref[2] = mul(x, blocks_ref[slot_of(list_ref, me, 17)]).astype(BF16)


def turn_body(x_ref, below_ref, from_right_ref, from_left_ref, rise_ref, sink_ref):
    rise_ref[0] = from_left_ref[0]
    rise_ref[1] = x_ref[...]
    rise_ref[2] = from_right_ref[0]
    sink_ref[...] = (
        below_ref[...].astype(F32) + from_left_ref[2].astype(F32) + from_right_ref[1].astype(F32)
    ).astype(BF16)


def near_body(me_ref, list_ref, x_ref, self_ref, blocks_ref, from_right_ref, from_left_ref, risen_ref, sunk_ref, out_ref):
    me = me_ref[0]
    total = mul_t(x_ref[...], self_ref[...])
    total += mul_t(from_right_ref[0], blocks_ref[slot_of(list_ref, me, 1)])
    total += mul_t(risen_ref[0], blocks_ref[slot_of(list_ref, me, 15)])
    total += mul_t(risen_ref[1], blocks_ref[slot_of(list_ref, me, 16)])
    total += mul_t(risen_ref[2], blocks_ref[slot_of(list_ref, me, 17)])
    out_ref[...] = total + from_left_ref[1].astype(F32) + sunk_ref[...].astype(F32)


def shards(
    right_sides,
    near_self,
    near_blocks,
    near_list,
    basis,
    transfer_one,
    transfer_two,
    couple_one,
    couple_two,
    far_list_one,
    far_list_two,
):
    me = lax.axis_index(AXES).astype(I32).reshape(1)
    x = right_sides[0, 0].T
    vectors = basis[0, 0].T
    one = transfer_one[0, 0]
    blocks = near_blocks[0, 0]
    links = near_list[0]

    message = call(
        up_body,
        shape(16, 128, 128),
        [pltpu.VMEM((2, PAD, 256), F32), pltpu.VMEM((8, 128), I32)],
        [VMEM] * 6,
        50 * 10**6,
        10**6,
    )(x, vectors, one, transfer_two[0, 0], far_list_one[0], far_list_two[0])
    got = lax.all_to_all(message, ("xh", "xl", "zl", "c"), 0, 0)
    window, level, lists = call(
        merge_body,
        (shape(RANK, 256), shape(RANK, RANK), shape(8, 128, dtype=I32)),
        [pltpu.VMEM((PAD, 256), F32), pltpu.VMEM((4, RANK, 256), F32)],
        [SMEM, VMEM],
        50 * 10**6,
        10**6,
    )(me, got)

    own = call(
        pack_body,
        shape(sum(SLOTS), RANK + PAD, 128),
        [pltpu.VMEM((RANK, 128), F32)],
        [VMEM] * 2,
        10**6,
        15 * 10**5,
    )(couple_one[0, 0], couple_two[0, 0])
    beside = lax.ppermute(own, "xl", [(0, 1), (1, 0)])
    across = lax.ppermute(jnp.concatenate([own, beside]), "c", [(0, 1), (1, 0)])

    left, right, below = call(
        mirror_body,
        (shape(2, 144, 512), shape(3, 144, 512), shape(144, 512)),
        [],
        [SMEM, SMEM, VMEM, VMEM],
        3 * 10**8,
        3 * 10**6,
    )(me, links, x, blocks)
    across_gy = ("zh", "zl", "c")
    along_gx = ("y", "xh", "xl")
    from_right = lax.ppermute(left, across_gy, [(i + 1, i) for i in range(15)])
    from_left = lax.ppermute(right, across_gy, [(i, i + 1) for i in range(15)])
    rise, sink = call(
        turn_body, (shape(3, 144, 512), shape(144, 512)), [], [VMEM] * 4, 10**6, 2 * 10**6
    )(x, below, from_right, from_left)
    risen = lax.ppermute(rise, along_gx, [(i + 1, i) for i in range(31)])
    sunk = lax.ppermute(sink, along_gx, [(i, i + 1) for i in range(31)])

    plane = lax.all_gather(window, "zh")
    above = lax.ppermute(plane, "y", [(i, i + 1) for i in range(7)])
    under = lax.ppermute(plane, "y", [(i + 1, i) for i in range(7)])

    near = call(
        near_body,
        shape(144, 512, dtype=F32),
        [],
        [SMEM, SMEM] + [VMEM] * 7,
        4 * 10**8,
        4 * 10**6,
    )(me, links, x, near_self[0, 0], blocks, from_right, from_left, risen, sunk)

    partial = call(
        couple_body,
        shape(8, 128, 128),
        [
            pltpu.VMEM((3, 4, RANK, 256), BF16),
            pltpu.VMEM((RANK, 256), F32),
            pltpu.VMEM((RANK, 256), F32),
            pltpu.VMEM((2, PAD, 256), F32),
        ],
        [SMEM, SMEM] + [VMEM] * 6,
        6 * 10**8,
        4 * 10**6,
    )(me, lists, above, plane, under, own, beside, across)
    sums = lax.all_to_all(partial, ("xl", "zl", "c"), 0, 0)
    applied = call(
        down_body,
        shape(144, 512),
        [pltpu.VMEM((PAD, 256), F32), pltpu.VMEM((RANK, RANK), F32)],
        [SMEM] + [VMEM] * 5,
        50 * 10**6,
        10**6,
    )(me, sums, level, one, vectors, near)
    return applied.T[None, None]


def solution(mesh):
    split = Mesh(mesh.devices.reshape(8, 2, 2, 4, 2, 2), AXES)
    rows, cols = AXES[:3], AXES[3:]

    def spec(rank):
        return P(rows, cols, *[None] * (rank - 2))

    ranks = (4, 4, 5, 3, 4, 4, 4, 5, 5, 3, 3)
    return jax.shard_map(
        shards, mesh=split, in_specs=tuple(map(spec, ranks)), out_specs=spec(4), check_vma=False
    )
```

```python
import functools

import jax
import jax.numpy as jnp
from jax import lax
from jax.experimental import pallas as pl
from jax.experimental.pallas import tpu as pltpu
from jax.sharding import Mesh, PartitionSpec as P

AXES = ("y", "xh", "xl", "zh", "zl", "c")
F32, BF16, I32 = jnp.float32, jnp.bfloat16, jnp.int32
RANK, CHUNK, PAD = 160, 36, 40
SLOTS = (7, 4)
VMEM = pl.BlockSpec(memory_space=pltpu.VMEM)
SMEM = pl.BlockSpec(memory_space=pltpu.SMEM)
ANY = pl.BlockSpec(memory_space=pl.ANY)
SLABS = 8


class Stage:
    def __init__(self, body, outs, scratch, args, lists=(), scalars=(), repeats=None):
        self.body, self.outs, self.scratch, self.args = body, outs, scratch, list(args)
        self.lists, self.scalars, self.repeats = list(lists), list(scalars), repeats or {}
        self.ready = [
            shape(max(self.repeats[o]) + 1, *out.shape[1:], dtype=out.dtype) if o in self.repeats else out
            for o, out in enumerate(outs)
        ]


def fused(*stages, flops=10**8, limit=60):
    shared = []

    def index(array):
        for i, held in enumerate(shared):
            if held is array:
                return i
        shared.append(array)
        return len(shared) - 1

    uses = [[index(a) for a in stage.args] for stage in stages]
    lists = [a for stage in stages for a in stage.lists]
    scalars = [a for stage in stages for a in stage.scalars]
    outs = [o for stage in stages for o in stage.outs]
    ready = [o for stage in stages for o in stage.ready]
    n_copies = sum(len(stage.repeats.get(o, (0,))) for stage in stages for o in range(len(stage.outs)))

    def run(*refs):
        refs = list(refs)

        def take(n):
            taken = refs[:n]
            del refs[:n]
            return taken

        ins, tables, plain, results = take(len(shared)), take(len(lists)), take(len(scalars)), take(len(outs))
        held, read, buffers, in_sems, out_sems = take(len(shared)), take(len(lists)), take(len(outs)), *take(2)
        fetch = [
            pltpu.make_async_copy(source, target, in_sems.at[i])
            for i, (source, target) in enumerate(zip(ins + tables, held + read))
        ]
        for copy in fetch:
            copy.start()
        for copy in fetch[len(shared) :]:
            copy.wait()
        arrived, leaving = set(), []
        for stage, use in zip(stages, uses):
            for i in use:
                if i not in arrived:
                    fetch[i].wait()
                    arrived.add(i)
            mine = [buffers.pop(0) for _ in stage.outs]
            targets = [results.pop(0) for _ in stage.outs]
            heads = [plain.pop(0) for _ in stage.scalars] + [read.pop(0) for _ in stage.lists]
            stage.body(*heads, *[held[i] for i in use], *mine, *take(len(stage.scratch)))
            for o in range(len(stage.outs)):
                pairs = [(mine[o], targets[o])]
                if o in stage.repeats:
                    pairs = [(mine[o].at[part], targets[o].at[d]) for d, part in enumerate(stage.repeats[o])]
                for source, target in pairs:
                    leaving.append(pltpu.make_async_copy(source, target, out_sems.at[len(leaving)]))
                    leaving[-1].start()
        for copy in leaving:
            copy.wait()

    buffers = [pltpu.VMEM(a.shape, a.dtype) for a in shared]
    buffers += [pltpu.SMEM(a.shape, a.dtype) for a in lists]
    buffers += [pltpu.VMEM(a.shape, a.dtype) for a in ready]
    buffers += [pltpu.SemaphoreType.DMA((len(shared) + len(lists),)), pltpu.SemaphoreType.DMA((n_copies,))]
    moved = sum(a.size * a.dtype.itemsize for a in [*shared, *outs])
    return pl.pallas_call(
        run,
        out_shape=outs,
        in_specs=[ANY] * (len(shared) + len(lists)) + [SMEM] * len(scalars),
        out_specs=[ANY] * len(outs),
        scratch_shapes=buffers + [b for stage in stages for b in stage.scratch],
        compiler_params=pltpu.CompilerParams(vmem_limit_bytes=limit * 2**20),
        cost_estimate=pl.CostEstimate(flops=flops, bytes_accessed=moved, transcendentals=0),
    )(*shared, *lists, *scalars)


def call(body, outs, scratch, specs, flops, moved):
    return pl.pallas_call(
        body,
        out_shape=outs,
        in_specs=specs,
        out_specs=jax.tree.map(lambda _: VMEM, outs),
        scratch_shapes=scratch,
        compiler_params=pltpu.CompilerParams(vmem_limit_bytes=16 * 2**20),
        cost_estimate=pl.CostEstimate(flops=flops, bytes_accessed=moved, transcendentals=0),
    )


def after(value, *others):
    return lax.optimization_barrier((value, *others))[0]


def shape(*dims, dtype=BF16):
    return jax.ShapeDtypeStruct(dims, dtype)


def mul(a, b):
    return lax.dot_general(a, b, (((1,), (0,)), ((), ())), preferred_element_type=F32)


def mul_t(a, b):
    return lax.dot_general(a, b, (((1,), (1,)), ((), ())), preferred_element_type=F32)


def spreader(groups, cols, transposed=False):
    dims = (cols, groups * PAD) if transposed else (groups * PAD, cols)
    padded = lax.broadcasted_iota(I32, dims, 1 if transposed else 0)
    dense = lax.broadcasted_iota(I32, dims, 0 if transposed else 1)
    hit = jnp.zeros(dims, jnp.bool_)
    for g in range(groups):
        inside = (padded >= PAD * g) & (padded < PAD * g + CHUNK)
        hit = hit | (inside & (dense == padded - (PAD - CHUNK) * g))
    return jnp.where(hit, 1.0, 0.0).astype(BF16)


def packed(a, b, tail, wide):
    wide[0, :, :RANK] = a
    wide[1, :, :RANK] = b
    rest = wide[0, :, 128:] + pltpu.roll(wide[1, :, 128:], 32, 1)
    return jnp.concatenate([wide[0, :, :128], wide[1, :, :128], rest, tail], axis=0).astype(BF16)


def up_body(far_one_ref, far_two_ref, x_ref, basis_ref, one_ref, two_ref, out_ref, wide):
    wide[...] = jnp.zeros_like(wide)
    row = lax.broadcasted_iota(I32, (8, 128), 0)
    lane = lax.broadcasted_iota(I32, (8, 128), 1)
    tail = jnp.full((8, 128), -1.0, F32)
    for r, ref in enumerate((far_one_ref, far_two_ref)):
        for k in range(SLOTS[r]):
            tail = jnp.where((row == r) & (lane == k), ref[0, k].astype(F32), tail)
    leaf = mul_t(x_ref[...], basis_ref[...]).astype(BF16)
    up = mul(leaf, one_ref[...]).astype(BF16)
    chunks = mul(spreader(4, 144), up)
    quarter = two_ref[...].astype(F32)
    for q in range(4):
        out_ref[q] = packed(chunks[PAD * q : PAD * (q + 1)], quarter, tail, wide)


def merge_body(me_ref, got_ref, window_ref, level_ref, lists_ref, wide, levels):
    me = me_ref[0]
    own = (me // 32) % 2 * 2 + me // 2 % 2
    lane = lax.broadcasted_iota(I32, (PAD, 128), 1)
    rests = [jnp.zeros((PAD, 128), F32)] * 2

    def deposit(level, place, main, rest):
        window_ref[0, 5 * level + place] = main.astype(BF16)
        rest = jnp.where(lane < 32, rest, 0.0)
        rests[level] = rests[level] + (pltpu.roll(rest, 32 * place, 1) if place else rest)

    for xh in range(2):
        second = jnp.zeros((PAD, RANK), F32)
        for zl in range(2):
            main = jnp.zeros((PAD, 128), F32)
            rest = jnp.zeros((PAD, 128), F32)
            for q in range(4):
                block = got_ref[xh * 8 + (q // 2) * 4 + zl * 2 + q % 2].astype(F32)
                main += block[:PAD]
                rest += block[2 * PAD : 3 * PAD]
                rows = slice(PAD * q, PAD * (q + 1))
                levels[xh * 2 + zl, rows, :128] = block[PAD : 2 * PAD]
                levels[xh * 2 + zl, rows, 128:] = pltpu.roll(block[2 * PAD : 3 * PAD], 96, 1)
            wide[:, :128] = main
            wide[:, 128:] = rest
            first = wide[:, :RANK]
            deposit(0, xh * 2 + zl, main, rest)
            second += mul(first.astype(BF16), levels[xh * 2 + zl, :, :RANK].astype(BF16))
        wide[:, :RANK] = second
        deposit(1, xh, wide[:, :128], wide[:, 128:])
    window_ref[0, 4] = rests[0].astype(BF16)
    window_ref[0, 7] = rests[1].astype(BF16)
    level_ref[...] = levels[own, :, :RANK].astype(BF16)
    for q in range(4):
        place = (me // 32) % 2 * 8 + (q // 2) * 4 + me // 2 % 2 * 2 + q % 2
        tail = got_ref[place, 112:, :].astype(F32)
        lists_ref[q : q + 1, :] = tail[8:9].astype(I32)
        lists_ref[4 + q : 5 + q, :] = tail[9:10].astype(I32)


def pack_body(one_ref, two_ref, out_ref, wide):
    wide[...] = jnp.zeros_like(wide)
    for g in range(3):
        rest = jnp.zeros((RANK, 128), F32)
        for s in range(4):
            lanes = slice(128 * s, 128 * (s + 1))
            if 4 * g + s == SLOTS[0]:
                out_ref[g, :, lanes] = jnp.zeros((RANK, 128), BF16)
                continue
            block = one_ref[4 * g + s] if g < 2 else two_ref[s]
            out_ref[g, :, lanes] = block[:, :128]
            wide[:, :32] = block[:, 128:].astype(F32)
            rest += wide[...] if s == 0 else pltpu.roll(wide[...], 32 * s, 1)
        out_ref[g, :, 512:] = rest.astype(BF16)


def couple_body(me_ref, lists_ref, up_ref, mid_ref, down_ref, own_ref, beside_ref, across_ref, opposite_ref, out_ref, rows, stack, wide):
    me = me_ref[0]
    y = me // 64
    q_own = me // 16 % 2 * 2 + me % 2
    rows[0] = up_ref[...]
    rows[1] = mid_ref[...]
    rows[2] = down_ref[...]
    lane = lax.broadcasted_iota(I32, (PAD, 128), 1)
    sources = ((own_ref, q_own), (beside_ref, q_own ^ 2), (across_ref, q_own ^ 1), (opposite_ref, q_own ^ 3))
    totals = [jnp.zeros((PAD, RANK), F32)] * 2
    for g in range(3):
        level = g // 2
        for which, (ref, q) in enumerate(sources):
            rest = jnp.zeros((PAD, 128), F32)
            for s in range(4):
                if 4 * g + s == SLOTS[0]:
                    stack[which, g, :, 128 * s : 128 * (s + 1)] = jnp.zeros((PAD, 128), BF16)
                    continue
                code = lists_ref[4 + q, s] if level else lists_ref[q, 4 * g + s]
                valid = code >= 0
                safe = jnp.where(valid, code, y * (8 if level else 16))
                row, col = (safe // 4, safe % 4) if level else (safe // 8, safe % 8)
                zh, place = (col, row % 2) if level else (col // 2, row % 2 * 2 + col % 2)
                plane = row // 2 - y + 1
                main = rows[plane, zh, 5 * level + place].astype(F32)
                stack[which, g, :, 128 * s : 128 * (s + 1)] = jnp.where(valid, main, 0.0).astype(BF16)
                turned = pltpu.roll(rows[plane, zh, 4 + 3 * level].astype(F32), (s + 4 - place) % 4 * 32, 1)
                inside = (lane >= 32 * s) & (lane < jnp.where(valid, 32 * (s + 1), 0))
                rest = jnp.where(inside, turned, rest)
            stack[which, g, :, 512:] = rest.astype(BF16)
            totals[level] = totals[level] + mul_t(stack[which, g], ref[g])
    wide[...] = jnp.zeros_like(wide)
    block = packed(totals[0], totals[1], jnp.zeros((8, 128), F32), wide)
    for d in range(8):
        out_ref[d] = block


def down_body(me_ref, got_ref, level_ref, one_ref, basis_ref, near_ref, out_ref, wide, local):
    me = me_ref[0]
    zl_own = me // 2 % 2
    for q in range(4):
        base = q // 2 * 4 + q % 2
        mine = got_ref[base + zl_own * 2].astype(F32)
        both = got_ref[base].astype(F32) + got_ref[base + 2].astype(F32)
        wide[:, :128] = both[PAD : 2 * PAD]
        wide[:, 128:] = pltpu.roll(both[2 * PAD : 3 * PAD], 96, 1)
        second = wide[:, :RANK].astype(BF16)
        wide[:, :128] = mine[:PAD]
        wide[:, 128:] = mine[2 * PAD : 3 * PAD]
        local[PAD * q : PAD * (q + 1), :] = wide[:, :RANK] + mul_t(second, level_ref[...])
    one = mul(spreader(4, 144, True), local[...].astype(BF16)).astype(BF16)
    leaf = mul_t(one, one_ref[...]).astype(BF16)
    out_ref[...] = (near_ref[...] + mul(leaf, basis_ref[...])).astype(BF16)


def slot_of(list_ref, me, apart):
    found = jnp.int32(0)
    for k in range(1, 4):
        found = jnp.where(list_ref[0, k] == me + apart, k, found)
    return found


def mirror_body(me_ref, list_ref, x_ref, blocks_ref, left_ref, right_ref, below_ref):
    me = me_ref[0]
    x = x_ref[...]
    left_ref[0] = x
    right_ref[0] = x
    right_ref[1] = mul(x, blocks_ref[slot_of(list_ref, me, 1)]).astype(BF16)
    left_ref[1] = mul(x, blocks_ref[slot_of(list_ref, me, 15)]).astype(BF16)
    below_ref[...] = mul(x, blocks_ref[slot_of(list_ref, me, 16)]).astype(BF16)
    right_ref[2] = mul(x, blocks_ref[slot_of(list_ref, me, 17)]).astype(BF16)


def turn_body(x_ref, below_ref, from_right_ref, from_left_ref, rise_ref, sink_ref):
    rise_ref[0] = from_left_ref[0]
    rise_ref[1] = x_ref[...]
    rise_ref[2] = from_right_ref[0]
    sink_ref[...] = (
        below_ref[...].astype(F32) + from_left_ref[2].astype(F32) + from_right_ref[1].astype(F32)
    ).astype(BF16)


def near_body(me_ref, list_ref, x_ref, self_ref, blocks_ref, from_right_ref, from_left_ref, risen_ref, sunk_ref, out_ref):
    me = me_ref[0]
    total = mul_t(x_ref[...], self_ref[...])
    total += mul_t(from_right_ref[0], blocks_ref[slot_of(list_ref, me, 1)])
    total += mul_t(risen_ref[0], blocks_ref[slot_of(list_ref, me, 15)])
    total += mul_t(risen_ref[1], blocks_ref[slot_of(list_ref, me, 16)])
    total += mul_t(risen_ref[2], blocks_ref[slot_of(list_ref, me, 17)])
    out_ref[...] = total + from_left_ref[1].astype(F32) + sunk_ref[...].astype(F32)


def shards(
    right_sides,
    near_self,
    near_blocks,
    near_list,
    basis,
    transfer_one,
    transfer_two,
    couple_one,
    couple_two,
    far_list_one,
    far_list_two,
):
    me = lax.axis_index(AXES).astype(I32).reshape(1)
    x = right_sides[0, 0].T
    vectors = basis[0, 0].T
    one = transfer_one[0, 0]
    blocks = near_blocks[0, 0]
    links = near_list[0]

    across_gy = ("zh", "zl", "c")
    along_gx = ("y", "xh", "xl")
    swap = [(0, 1), (1, 0)]

    message, left, right, below, own = fused(
        Stage(
            up_body,
            [shape(16, 128, 128)],
            [pltpu.VMEM((2, PAD, 256), F32)],
            [x, vectors, one, transfer_two[0, 0]],
            lists=[far_list_one[0], far_list_two[0]],
            repeats={0: [d // 4 % 2 * 2 + d % 2 for d in range(16)]},
        ),
        Stage(
            mirror_body,
            [shape(2, 144, 512), shape(3, 144, 512), shape(144, 512)],
            [],
            [x, blocks],
            lists=[links],
            scalars=[me],
        ),
        Stage(
            pack_body, [shape(3, RANK, 640)], [pltpu.VMEM((RANK, 128), F32)], [couple_one[0, 0], couple_two[0, 0]]
        ),
        flops=4 * 10**8,
    )
    got = lax.all_to_all(message, ("xh", "xl", "zl", "c"), 0, 0)
    from_right = lax.ppermute(left, across_gy, [(i + 1, i) for i in range(15)])
    from_left = lax.ppermute(right, across_gy, [(i, i + 1) for i in range(15)])
    beside = lax.ppermute(own, "xl", swap)
    across = lax.ppermute(own, "c", swap)
    got, across = lax.optimization_barrier((got, across))
    window, level, codes, rise, sink = fused(
        Stage(
            merge_body,
            [shape(4, SLABS, PAD, 128), shape(RANK, RANK), shape(8, 128, dtype=I32)],
            [pltpu.VMEM((PAD, 256), F32), pltpu.VMEM((4, RANK, 256), F32)],
            [got],
            scalars=[me],
            repeats={0: [0] * 4},
        ),
        Stage(
            turn_body, [shape(3, 144, 512), shape(144, 512)], [], [x, below, from_right, from_left]
        ),
    )
    plane = lax.all_to_all(window, "zh", 0, 0)
    risen = lax.ppermute(rise, along_gx, [(i + 1, i) for i in range(31)])
    sunk = lax.ppermute(sink, along_gx, [(i, i + 1) for i in range(31)])

    plane, beside, risen, sunk = lax.optimization_barrier((plane, beside, risen, sunk))
    opposite = lax.ppermute(beside, "c", swap)
    above = lax.ppermute(plane, "y", [(i, i + 1) for i in range(7)])
    under = lax.ppermute(plane, "y", [(i + 1, i) for i in range(7)])
    near = call(
        near_body, shape(144, 512, dtype=F32), [], [SMEM, SMEM] + [VMEM] * 7, 4 * 10**8, 4 * 10**6
    )(me, links, x, near_self[0, 0], blocks, from_right, from_left, risen, sunk)
    codes = after(codes, near)
    partial = call(
        couple_body,
        shape(8, 128, 128),
        [
            pltpu.VMEM((3, 4, SLABS, PAD, 128), BF16),
            pltpu.VMEM((4, 3, PAD, 640), BF16),
            pltpu.VMEM((2, PAD, 256), F32),
        ],
        [SMEM, SMEM] + [VMEM] * 7,
        6 * 10**8,
        4 * 10**6,
    )(me, codes, above, plane, under, own, beside, across, opposite)
    sums = lax.all_to_all(partial, ("xl", "zl", "c"), 0, 0)
    applied = call(
        down_body,
        shape(144, 512),
        [pltpu.VMEM((PAD, 256), F32), pltpu.VMEM((RANK, RANK), F32)],
        [SMEM] + [VMEM] * 5,
        10**8,
        10**6,
    )(me, sums, level, one, vectors, near)
    return applied.T[None, None]


def solution(mesh):
    split = Mesh(mesh.devices.reshape(8, 2, 2, 4, 2, 2), AXES)
    rows, cols = AXES[:3], AXES[3:]

    def spec(rank):
        return P(rows, cols, *[None] * (rank - 2))

    ranks = (4, 4, 5, 3, 4, 4, 4, 5, 5, 3, 3)
    return jax.shard_map(
        shards, mesh=split, in_specs=tuple(map(spec, ranks)), out_specs=spec(4), check_vma=False
    )
```

```python
import functools

import jax
import jax.numpy as jnp
from jax import lax
from jax.experimental import pallas as pl
from jax.experimental.pallas import tpu as pltpu
from jax.sharding import Mesh, PartitionSpec as P

AXES = ("y", "xh", "xl", "zh", "zl", "c")
F32, BF16, I32 = jnp.float32, jnp.bfloat16, jnp.int32
RANK, CHUNK, PAD = 160, 36, 40
SLOTS = (7, 4)
VMEM = pl.BlockSpec(memory_space=pltpu.VMEM)
SMEM = pl.BlockSpec(memory_space=pltpu.SMEM)
ANY = pl.BlockSpec(memory_space=pl.ANY)
SLABS = 8


class Stage:
    def __init__(self, body, outs, scratch, args, lists=(), scalars=(), repeats=None):
        self.body, self.outs, self.scratch, self.args = body, outs, scratch, list(args)
        self.lists, self.scalars, self.repeats = list(lists), list(scalars), repeats or {}
        self.ready = [
            shape(max(self.repeats[o]) + 1, *out.shape[1:], dtype=out.dtype) if o in self.repeats else out
            for o, out in enumerate(outs)
        ]


def fused(*stages, flops=10**8, limit=60):
    shared = []

    def index(array):
        for i, held in enumerate(shared):
            if held is array:
                return i
        shared.append(array)
        return len(shared) - 1

    uses = [[index(a) for a in stage.args] for stage in stages]
    lists = [a for stage in stages for a in stage.lists]
    scalars = [a for stage in stages for a in stage.scalars]
    outs = [o for stage in stages for o in stage.outs]
    ready = [o for stage in stages for o in stage.ready]
    n_copies = sum(len(stage.repeats.get(o, (0,))) for stage in stages for o in range(len(stage.outs)))

    def run(*refs):
        refs = list(refs)

        def take(n):
            taken = refs[:n]
            del refs[:n]
            return taken

        ins, tables, plain, results = take(len(shared)), take(len(lists)), take(len(scalars)), take(len(outs))
        held, read, buffers, in_sems, out_sems = take(len(shared)), take(len(lists)), take(len(outs)), *take(2)
        fetch = [
            pltpu.make_async_copy(source, target, in_sems.at[i])
            for i, (source, target) in enumerate(zip(ins + tables, held + read))
        ]
        for copy in fetch:
            copy.start()
        for copy in fetch[len(shared) :]:
            copy.wait()
        arrived, leaving = set(), []
        for stage, use in zip(stages, uses):
            for i in use:
                if i not in arrived:
                    fetch[i].wait()
                    arrived.add(i)
            mine = [buffers.pop(0) for _ in stage.outs]
            targets = [results.pop(0) for _ in stage.outs]
            heads = [plain.pop(0) for _ in stage.scalars] + [read.pop(0) for _ in stage.lists]
            stage.body(*heads, *[held[i] for i in use], *mine, *take(len(stage.scratch)))
            for o in range(len(stage.outs)):
                pairs = [(mine[o], targets[o])]
                if o in stage.repeats:
                    pairs = [(mine[o].at[part], targets[o].at[d]) for d, part in enumerate(stage.repeats[o])]
                for source, target in pairs:
                    leaving.append(pltpu.make_async_copy(source, target, out_sems.at[len(leaving)]))
                    leaving[-1].start()
        for copy in leaving:
            copy.wait()

    buffers = [pltpu.VMEM(a.shape, a.dtype) for a in shared]
    buffers += [pltpu.SMEM(a.shape, a.dtype) for a in lists]
    buffers += [pltpu.VMEM(a.shape, a.dtype) for a in ready]
    buffers += [pltpu.SemaphoreType.DMA((len(shared) + len(lists),)), pltpu.SemaphoreType.DMA((n_copies,))]
    moved = sum(a.size * a.dtype.itemsize for a in [*shared, *outs])
    return pl.pallas_call(
        run,
        out_shape=outs,
        in_specs=[ANY] * (len(shared) + len(lists)) + [SMEM] * len(scalars),
        out_specs=[ANY] * len(outs),
        scratch_shapes=buffers + [b for stage in stages for b in stage.scratch],
        compiler_params=pltpu.CompilerParams(vmem_limit_bytes=limit * 2**20),
        cost_estimate=pl.CostEstimate(flops=flops, bytes_accessed=moved, transcendentals=0),
    )(*shared, *lists, *scalars)


def call(body, outs, scratch, specs, flops, moved):
    return pl.pallas_call(
        body,
        out_shape=outs,
        in_specs=specs,
        out_specs=jax.tree.map(lambda _: VMEM, outs),
        scratch_shapes=scratch,
        compiler_params=pltpu.CompilerParams(vmem_limit_bytes=16 * 2**20),
        cost_estimate=pl.CostEstimate(flops=flops, bytes_accessed=moved, transcendentals=0),
    )


def after(value, *others):
    return lax.optimization_barrier((value, *others))[0]


def shape(*dims, dtype=BF16):
    return jax.ShapeDtypeStruct(dims, dtype)


def mul(a, b):
    return lax.dot_general(a, b, (((1,), (0,)), ((), ())), preferred_element_type=F32)


def mul_t(a, b):
    return lax.dot_general(a, b, (((1,), (1,)), ((), ())), preferred_element_type=F32)


def spreader(groups, cols, transposed=False):
    dims = (cols, groups * PAD) if transposed else (groups * PAD, cols)
    padded = lax.broadcasted_iota(I32, dims, 1 if transposed else 0)
    dense = lax.broadcasted_iota(I32, dims, 0 if transposed else 1)
    hit = jnp.zeros(dims, jnp.bool_)
    for g in range(groups):
        inside = (padded >= PAD * g) & (padded < PAD * g + CHUNK)
        hit = hit | (inside & (dense == padded - (PAD - CHUNK) * g))
    return jnp.where(hit, 1.0, 0.0).astype(BF16)


def packed(a, b, tail, wide):
    wide[0, :, :RANK] = a
    wide[1, :, :RANK] = b
    rest = wide[0, :, 128:] + pltpu.roll(wide[1, :, 128:], 32, 1)
    return jnp.concatenate([wide[0, :, :128], wide[1, :, :128], rest, tail], axis=0).astype(BF16)


def up_body(far_one_ref, far_two_ref, x_ref, basis_ref, one_ref, two_ref, out_ref, wide):
    wide[...] = jnp.zeros_like(wide)
    row = lax.broadcasted_iota(I32, (8, 128), 0)
    lane = lax.broadcasted_iota(I32, (8, 128), 1)
    tail = jnp.full((8, 128), -1.0, F32)
    for r, ref in enumerate((far_one_ref, far_two_ref)):
        for k in range(SLOTS[r]):
            tail = jnp.where((row == r) & (lane == k), ref[0, k].astype(F32), tail)
    leaf = mul_t(x_ref[...], basis_ref[...]).astype(BF16)
    up = mul(leaf, one_ref[...]).astype(BF16)
    chunks = mul(spreader(4, 144), up)
    quarter = two_ref[...].astype(F32)
    for q in range(4):
        out_ref[q] = packed(chunks[PAD * q : PAD * (q + 1)], quarter, tail, wide)


def merge_body(me_ref, got_ref, window_ref, level_ref, lists_ref, wide, levels):
    me = me_ref[0]
    own = (me // 32) % 2 * 2 + me // 2 % 2
    lane = lax.broadcasted_iota(I32, (PAD, 128), 1)
    rests = [jnp.zeros((PAD, 128), F32)] * 2

    def deposit(level, place, main, rest):
        window_ref[0, 5 * level + place] = main.astype(BF16)
        rest = jnp.where(lane < 32, rest, 0.0)
        rests[level] = rests[level] + (pltpu.roll(rest, 32 * place, 1) if place else rest)

    for xh in range(2):
        second = jnp.zeros((PAD, RANK), F32)
        for zl in range(2):
            main = jnp.zeros((PAD, 128), F32)
            rest = jnp.zeros((PAD, 128), F32)
            for q in range(4):
                block = got_ref[xh * 8 + (q // 2) * 4 + zl * 2 + q % 2].astype(F32)
                main += block[:PAD]
                rest += block[2 * PAD : 3 * PAD]
                rows = slice(PAD * q, PAD * (q + 1))
                levels[xh * 2 + zl, rows, :128] = block[PAD : 2 * PAD]
                levels[xh * 2 + zl, rows, 128:] = pltpu.roll(block[2 * PAD : 3 * PAD], 96, 1)
            wide[:, :128] = main
            wide[:, 128:] = rest
            first = wide[:, :RANK]
            deposit(0, xh * 2 + zl, main, rest)
            second += mul(first.astype(BF16), levels[xh * 2 + zl, :, :RANK].astype(BF16))
        wide[:, :RANK] = second
        deposit(1, xh, wide[:, :128], wide[:, 128:])
    window_ref[0, 4] = rests[0].astype(BF16)
    window_ref[0, 7] = rests[1].astype(BF16)
    level_ref[...] = levels[own, :, :RANK].astype(BF16)
    for q in range(4):
        place = (me // 32) % 2 * 8 + (q // 2) * 4 + me // 2 % 2 * 2 + q % 2
        tail = got_ref[place, 112:, :].astype(F32)
        lists_ref[q : q + 1, :] = tail[8:9].astype(I32)
        lists_ref[4 + q : 5 + q, :] = tail[9:10].astype(I32)


def pack_body(one_ref, two_ref, out_ref, wide):
    wide[...] = jnp.zeros_like(wide)
    for g in range(3):
        rest = jnp.zeros((RANK, 128), F32)
        for s in range(4):
            lanes = slice(128 * s, 128 * (s + 1))
            if 4 * g + s == SLOTS[0]:
                out_ref[g, :, lanes] = jnp.zeros((RANK, 128), BF16)
                continue
            block = one_ref[4 * g + s] if g < 2 else two_ref[s]
            out_ref[g, :, lanes] = block[:, :128]
            wide[:, :32] = block[:, 128:].astype(F32)
            rest += wide[...] if s == 0 else pltpu.roll(wide[...], 32 * s, 1)
        out_ref[g, :, 512:] = rest.astype(BF16)


def couple_body(me_ref, lists_ref, up_ref, mid_ref, down_ref, own_ref, beside_ref, across_ref, opposite_ref, out_ref, rows, stack, wide):
    me = me_ref[0]
    y = me // 64
    q_own = me // 16 % 2 * 2 + me % 2
    rows[0] = up_ref[...]
    rows[1] = mid_ref[...]
    rows[2] = down_ref[...]
    lane = lax.broadcasted_iota(I32, (PAD, 128), 1)
    sources = ((own_ref, q_own), (beside_ref, q_own ^ 2), (across_ref, q_own ^ 1), (opposite_ref, q_own ^ 3))
    totals = [jnp.zeros((PAD, RANK), F32)] * 2
    for g in range(3):
        level = g // 2
        for which, (ref, q) in enumerate(sources):
            rest = jnp.zeros((PAD, 128), F32)
            for s in range(4):
                if 4 * g + s == SLOTS[0]:
                    stack[which, g, :, 128 * s : 128 * (s + 1)] = jnp.zeros((PAD, 128), BF16)
                    continue
                code = lists_ref[4 + q, s] if level else lists_ref[q, 4 * g + s]
                valid = code >= 0
                safe = jnp.where(valid, code, y * (8 if level else 16))
                row, col = (safe // 4, safe % 4) if level else (safe // 8, safe % 8)
                zh, place = (col, row % 2) if level else (col // 2, row % 2 * 2 + col % 2)
                plane = row // 2 - y + 1
                main = rows[plane, zh, 5 * level + place].astype(F32)
                stack[which, g, :, 128 * s : 128 * (s + 1)] = jnp.where(valid, main, 0.0).astype(BF16)
                turned = pltpu.roll(rows[plane, zh, 4 + 3 * level].astype(F32), (s + 4 - place) % 4 * 32, 1)
                inside = (lane >= 32 * s) & (lane < jnp.where(valid, 32 * (s + 1), 0))
                rest = jnp.where(inside, turned, rest)
            stack[which, g, :, 512:] = rest.astype(BF16)
            totals[level] = totals[level] + mul_t(stack[which, g], ref[g])
    wide[...] = jnp.zeros_like(wide)
    block = packed(totals[0], totals[1], jnp.zeros((8, 128), F32), wide)
    for d in range(8):
        out_ref[d] = block


def down_body(me_ref, got_ref, level_ref, one_ref, basis_ref, near_ref, out_ref, wide, local):
    me = me_ref[0]
    zl_own = me // 2 % 2
    for q in range(4):
        base = q // 2 * 4 + q % 2
        mine = got_ref[base + zl_own * 2].astype(F32)
        both = got_ref[base].astype(F32) + got_ref[base + 2].astype(F32)
        wide[:, :128] = both[PAD : 2 * PAD]
        wide[:, 128:] = pltpu.roll(both[2 * PAD : 3 * PAD], 96, 1)
        second = wide[:, :RANK].astype(BF16)
        wide[:, :128] = mine[:PAD]
        wide[:, 128:] = mine[2 * PAD : 3 * PAD]
        local[PAD * q : PAD * (q + 1), :] = wide[:, :RANK] + mul_t(second, level_ref[...])
    one = mul(spreader(4, 144, True), local[...].astype(BF16)).astype(BF16)
    leaf = mul_t(one, one_ref[...]).astype(BF16)
    out_ref[...] = (near_ref[...] + mul(leaf, basis_ref[...])).astype(BF16)


def slot_of(list_ref, me, apart):
    found = jnp.int32(0)
    for k in range(1, 4):
        found = jnp.where(list_ref[0, k] == me + apart, k, found)
    return found


def mirror_body(me_ref, list_ref, x_ref, blocks_ref, left_ref, right_ref, below_ref):
    me = me_ref[0]
    x = x_ref[...]
    left_ref[0] = x
    right_ref[0] = x
    right_ref[1] = mul(x, blocks_ref[slot_of(list_ref, me, 1)]).astype(BF16)
    left_ref[1] = mul(x, blocks_ref[slot_of(list_ref, me, 15)]).astype(BF16)
    below_ref[...] = mul(x, blocks_ref[slot_of(list_ref, me, 16)]).astype(BF16)
    right_ref[2] = mul(x, blocks_ref[slot_of(list_ref, me, 17)]).astype(BF16)


def turn_body(x_ref, below_ref, from_right_ref, from_left_ref, rise_ref, sink_ref):
    rise_ref[0] = from_left_ref[0]
    rise_ref[1] = x_ref[...]
    rise_ref[2] = from_right_ref[0]
    sink_ref[...] = (
        below_ref[...].astype(F32) + from_left_ref[2].astype(F32) + from_right_ref[1].astype(F32)
    ).astype(BF16)


def near_body(me_ref, list_ref, x_ref, self_ref, blocks_ref, from_right_ref, from_left_ref, risen_ref, sunk_ref, out_ref):
    me = me_ref[0]
    total = mul_t(x_ref[...], self_ref[...])
    total += mul_t(from_right_ref[0], blocks_ref[slot_of(list_ref, me, 1)])
    total += mul_t(risen_ref[0], blocks_ref[slot_of(list_ref, me, 15)])
    total += mul_t(risen_ref[1], blocks_ref[slot_of(list_ref, me, 16)])
    total += mul_t(risen_ref[2], blocks_ref[slot_of(list_ref, me, 17)])
    out_ref[...] = total + from_left_ref[1].astype(F32) + sunk_ref[...].astype(F32)


def shards(
    right_sides,
    near_self,
    near_blocks,
    near_list,
    basis,
    transfer_one,
    transfer_two,
    couple_one,
    couple_two,
    far_list_one,
    far_list_two,
):
    me = lax.axis_index(AXES).astype(I32).reshape(1)
    x = right_sides[0, 0].T
    vectors = basis[0, 0].T
    one = transfer_one[0, 0]
    blocks = near_blocks[0, 0]
    links = near_list[0]

    across_gy = ("zh", "zl", "c")
    along_gx = ("y", "xh", "xl")
    swap = [(0, 1), (1, 0)]

    message, left, right, below, own = fused(
        Stage(
            up_body,
            [shape(16, 128, 128)],
            [pltpu.VMEM((2, PAD, 256), F32)],
            [x, vectors, one, transfer_two[0, 0]],
            lists=[far_list_one[0], far_list_two[0]],
            repeats={0: [d // 4 % 2 * 2 + d % 2 for d in range(16)]},
        ),
        Stage(
            mirror_body,
            [shape(2, 144, 512), shape(3, 144, 512), shape(144, 512)],
            [],
            [x, blocks],
            lists=[links],
            scalars=[me],
        ),
        Stage(
            pack_body, [shape(3, RANK, 640)], [pltpu.VMEM((RANK, 128), F32)], [couple_one[0, 0], couple_two[0, 0]]
        ),
        flops=4 * 10**8,
    )
    got = lax.all_to_all(message, ("xh", "xl", "zl", "c"), 0, 0)
    from_right = lax.ppermute(left, across_gy, [(i + 1, i) for i in range(15)])
    from_left = lax.ppermute(right, across_gy, [(i, i + 1) for i in range(15)])
    beside = lax.ppermute(own, "xl", swap)
    window, level, codes = fused(
        Stage(
            merge_body,
            [shape(4, SLABS, PAD, 128), shape(RANK, RANK), shape(8, 128, dtype=I32)],
            [pltpu.VMEM((PAD, 256), F32), pltpu.VMEM((4, RANK, 256), F32)],
            [got],
            scalars=[me],
            repeats={0: [0] * 4},
        ),
    )
    plane = lax.all_to_all(window, "zh", 0, 0)
    below, late, _ = lax.optimization_barrier((below, own, window))
    rise, sink = fused(
        Stage(turn_body, [shape(3, 144, 512), shape(144, 512)], [], [x, below, from_right, from_left])
    )
    risen = lax.ppermute(rise, along_gx, [(i + 1, i) for i in range(31)])
    sunk = lax.ppermute(sink, along_gx, [(i, i + 1) for i in range(31)])
    across = lax.ppermute(late, "c", swap)
    beside, _ = lax.optimization_barrier((beside, plane))
    opposite = lax.ppermute(beside, "c", swap)
    above = lax.ppermute(plane, "y", [(i, i + 1) for i in range(7)])
    under = lax.ppermute(plane, "y", [(i + 1, i) for i in range(7)])
    near = call(
        near_body, shape(144, 512, dtype=F32), [], [SMEM, SMEM] + [VMEM] * 7, 5 * 10**9, 4 * 10**6
    )(me, links, x, near_self[0, 0], blocks, from_right, from_left, risen, sunk)
    codes = after(codes, near)
    partial = call(
        couple_body,
        shape(8, 128, 128),
        [
            pltpu.VMEM((3, 4, SLABS, PAD, 128), BF16),
            pltpu.VMEM((4, 3, PAD, 640), BF16),
            pltpu.VMEM((2, PAD, 256), F32),
        ],
        [SMEM, SMEM] + [VMEM] * 7,
        6 * 10**8,
        4 * 10**6,
    )(me, codes, above, plane, under, own, beside, across, opposite)
    sums = lax.all_to_all(partial, ("xl", "zl", "c"), 0, 0)
    applied = call(
        down_body,
        shape(144, 512),
        [pltpu.VMEM((PAD, 256), F32), pltpu.VMEM((RANK, RANK), F32)],
        [SMEM] + [VMEM] * 5,
        10**8,
        10**6,
    )(me, sums, level, one, vectors, near)
    return applied.T[None, None]


def solution(mesh):
    split = Mesh(mesh.devices.reshape(8, 2, 2, 4, 2, 2), AXES)
    rows, cols = AXES[:3], AXES[3:]

    def spec(rank):
        return P(rows, cols, *[None] * (rank - 2))

    ranks = (4, 4, 5, 3, 4, 4, 4, 5, 5, 3, 3)
    return jax.shard_map(
        shards, mesh=split, in_specs=tuple(map(spec, ranks)), out_specs=spec(4), check_vma=False
    )
```

```python
import functools

import jax
import jax.numpy as jnp
from jax import lax
from jax.experimental import pallas as pl
from jax.experimental.pallas import tpu as pltpu
from jax.sharding import Mesh, PartitionSpec as P

AXES = ("y", "xh", "xl", "zh", "zl", "c")
F32, BF16, I32 = jnp.float32, jnp.bfloat16, jnp.int32
RANK, CHUNK, PAD = 160, 36, 40
SLOTS = (7, 4)
VMEM = pl.BlockSpec(memory_space=pltpu.VMEM)
SMEM = pl.BlockSpec(memory_space=pltpu.SMEM)
ANY = pl.BlockSpec(memory_space=pl.ANY)
SLABS = 8


class Stage:
    def __init__(self, body, outs, scratch, args, lists=(), scalars=(), repeats=None, heads=None, also=()):
        self.body, self.outs, self.scratch, self.args = body, outs, scratch, list(args)
        self.lists, self.scalars, self.repeats = list(lists), list(scalars), repeats or {}
        self.heads, self.also = heads or {}, also
        self.ready = [
            shape(max(self.repeats[o]) + 1, *out.shape[1:], dtype=out.dtype)
            if o in self.repeats
            else shape(self.heads.get(o, out.shape[0]), *out.shape[1:], dtype=out.dtype)
            for o, out in enumerate(outs)
        ]


def fused(*stages, flops=10**8, limit=60):
    shared = []

    def index(array):
        for i, held in enumerate(shared):
            if held is array:
                return i
        shared.append(array)
        return len(shared) - 1

    uses = [[index(a) for a in stage.args] for stage in stages]
    lists = [a for stage in stages for a in stage.lists]
    scalars = [a for stage in stages for a in stage.scalars]
    outs = [o for stage in stages for o in stage.outs]
    ready = [o for stage in stages for o in stage.ready]
    n_copies = sum(len(stage.repeats.get(o, (0,))) for stage in stages for o in range(len(stage.outs)))
    n_copies += sum(len(stage.also) for stage in stages)

    def run(*refs):
        refs = list(refs)

        def take(n):
            taken = refs[:n]
            del refs[:n]
            return taken

        ins, tables, plain, results = take(len(shared)), take(len(lists)), take(len(scalars)), take(len(outs))
        held, read, buffers, in_sems, out_sems = take(len(shared)), take(len(lists)), take(len(outs)), *take(2)
        fetch = [
            pltpu.make_async_copy(source, target, in_sems.at[i])
            for i, (source, target) in enumerate(zip(ins + tables, held + read))
        ]
        for copy in fetch:
            copy.start()
        for copy in fetch[len(shared) :]:
            copy.wait()
        arrived, leaving, everything = set(), [], list(results)
        for stage, use in zip(stages, uses):
            for i in use:
                if i not in arrived:
                    fetch[i].wait()
                    arrived.add(i)
            mine = [buffers.pop(0) for _ in stage.outs]
            targets = [results.pop(0) for _ in stage.outs]
            heads = [plain.pop(0) for _ in stage.scalars] + [read.pop(0) for _ in stage.lists]
            stage.body(*heads, *[held[i] for i in use], *mine, *take(len(stage.scratch)))
            for o in range(len(stage.outs)):
                whole = targets[o].at[pl.ds(0, stage.heads[o])] if o in stage.heads else targets[o]
                pairs = [(mine[o], whole)]
                if o in stage.repeats:
                    pairs = [(mine[o].at[part], targets[o].at[d]) for d, part in enumerate(stage.repeats[o])]
                for held_at, out, row in stage.also:
                    if held_at == o:
                        pairs.append((mine[o], everything[out].at[pl.ds(row, mine[o].shape[0])]))
                for source, target in pairs:
                    leaving.append(pltpu.make_async_copy(source, target, out_sems.at[len(leaving)]))
                    leaving[-1].start()
        for copy in leaving:
            copy.wait()

    buffers = [pltpu.VMEM(a.shape, a.dtype) for a in shared]
    buffers += [pltpu.SMEM(a.shape, a.dtype) for a in lists]
    buffers += [pltpu.VMEM(a.shape, a.dtype) for a in ready]
    buffers += [pltpu.SemaphoreType.DMA((len(shared) + len(lists),)), pltpu.SemaphoreType.DMA((n_copies,))]
    moved = sum(a.size * a.dtype.itemsize for a in [*shared, *outs])
    return pl.pallas_call(
        run,
        out_shape=outs,
        in_specs=[ANY] * (len(shared) + len(lists)) + [SMEM] * len(scalars),
        out_specs=[ANY] * len(outs),
        scratch_shapes=buffers + [b for stage in stages for b in stage.scratch],
        compiler_params=pltpu.CompilerParams(vmem_limit_bytes=limit * 2**20),
        cost_estimate=pl.CostEstimate(flops=flops, bytes_accessed=moved, transcendentals=0),
    )(*shared, *lists, *scalars)


def call(body, outs, scratch, specs, flops, moved):
    return pl.pallas_call(
        body,
        out_shape=outs,
        in_specs=specs,
        out_specs=jax.tree.map(lambda _: VMEM, outs),
        scratch_shapes=scratch,
        compiler_params=pltpu.CompilerParams(vmem_limit_bytes=16 * 2**20),
        cost_estimate=pl.CostEstimate(flops=flops, bytes_accessed=moved, transcendentals=0),
    )


def after(value, *others):
    return lax.optimization_barrier((value, *others))[0]


def shape(*dims, dtype=BF16):
    return jax.ShapeDtypeStruct(dims, dtype)


def mul(a, b):
    return lax.dot_general(a, b, (((1,), (0,)), ((), ())), preferred_element_type=F32)


def mul_t(a, b):
    return lax.dot_general(a, b, (((1,), (1,)), ((), ())), preferred_element_type=F32)


def spreader(groups, cols, transposed=False):
    dims = (cols, groups * PAD) if transposed else (groups * PAD, cols)
    padded = lax.broadcasted_iota(I32, dims, 1 if transposed else 0)
    dense = lax.broadcasted_iota(I32, dims, 0 if transposed else 1)
    hit = jnp.zeros(dims, jnp.bool_)
    for g in range(groups):
        inside = (padded >= PAD * g) & (padded < PAD * g + CHUNK)
        hit = hit | (inside & (dense == padded - (PAD - CHUNK) * g))
    return jnp.where(hit, 1.0, 0.0).astype(BF16)


ROWS = 104


def packed(a, b, tail, wide):
    wide[0, :, :RANK] = a
    wide[1, :, :RANK] = b
    first, second = wide[0, :, 128:], wide[1, :, 128:]
    rest = (
        first[:24]
        + pltpu.roll(jnp.concatenate([first[24:], tail], axis=0), 32, 1)
        + pltpu.roll(second[:24], 64, 1)
        + pltpu.roll(jnp.concatenate([second[24:], jnp.zeros((8, 128), F32)], axis=0), 96, 1)
    )
    return jnp.concatenate([wide[0, :, :128], wide[1, :, :128], rest], axis=0).astype(BF16)


def rest_of(block, which):
    rest = block[2 * PAD :]
    left = pltpu.roll(rest, 64, 1) if which else rest
    return jnp.concatenate([left, pltpu.roll(left, 96, 1)[:16]], axis=0)


def up_body(far_one_ref, far_two_ref, x_ref, basis_ref, one_ref, two_ref, out_ref, wide):
    wide[...] = jnp.zeros_like(wide)
    row = lax.broadcasted_iota(I32, (8, 128), 0)
    lane = lax.broadcasted_iota(I32, (8, 128), 1)
    tail = jnp.full((8, 128), -1.0, F32)
    for r, ref in enumerate((far_one_ref, far_two_ref)):
        for k in range(SLOTS[r]):
            tail = jnp.where((row == r) & (lane == k), ref[0, k].astype(F32), tail)
    tail = jnp.where(lane < 32, tail, 0.0)
    leaf = mul_t(x_ref[...], basis_ref[...]).astype(BF16)
    up = mul(leaf, one_ref[...]).astype(BF16)
    chunks = mul(spreader(4, 144), up)
    quarter = two_ref[...].astype(F32)
    for q in range(4):
        out_ref[q] = packed(chunks[PAD * q : PAD * (q + 1)], quarter, tail, wide)


def merge_body(me_ref, got_ref, window_ref, level_ref, lists_ref, wide, levels):
    me = me_ref[0]
    own = (me // 32) % 2 * 2 + me // 2 % 2
    lane = lax.broadcasted_iota(I32, (PAD, 128), 1)
    rests = [jnp.zeros((PAD, 128), F32)] * 2

    def deposit(level, place, main, rest):
        window_ref[0, 5 * level + place] = main.astype(BF16)
        rest = jnp.where(lane < 32, rest, 0.0)
        rests[level] = rests[level] + (pltpu.roll(rest, 32 * place, 1) if place else rest)

    for xh in range(2):
        second = jnp.zeros((PAD, RANK), F32)
        for zl in range(2):
            total = jnp.zeros((ROWS, 128), F32)
            for q in range(4):
                block = got_ref[xh * 8 + (q // 2) * 4 + zl * 2 + q % 2].astype(F32)
                total += block
                rows = slice(PAD * q, PAD * (q + 1))
                levels[xh * 2 + zl, rows, :128] = block[PAD : 2 * PAD]
                levels[xh * 2 + zl, rows, 128:] = rest_of(block, 1)
            main, rest = total[:PAD], rest_of(total, 0)
            wide[:, :128] = main
            wide[:, 128:] = rest
            first = wide[:, :RANK]
            deposit(0, xh * 2 + zl, main, rest)
            second += mul(first.astype(BF16), levels[xh * 2 + zl, :, :RANK].astype(BF16))
        wide[:, :RANK] = second
        deposit(1, xh, wide[:, :128], wide[:, 128:])
    window_ref[0, 4] = rests[0].astype(BF16)
    window_ref[0, 7] = rests[1].astype(BF16)
    level_ref[...] = levels[own, :, :RANK].astype(BF16)
    for q in range(4):
        place = (me // 32) % 2 * 8 + (q // 2) * 4 + me // 2 % 2 * 2 + q % 2
        tail = pltpu.roll(got_ref[place].astype(F32)[2 * PAD :], 96, 1)
        lists_ref[q : q + 1, :] = tail[16:17].astype(I32)
        lists_ref[4 + q : 5 + q, :] = tail[17:18].astype(I32)


def couple_body(me_ref, lists_ref, up_ref, mid_ref, down_ref, own_ref, beside_ref, across_ref, opposite_ref, out_ref, rows, stack, wide):
    me = me_ref[0]
    y = me // 64
    q_own = me // 16 % 2 * 2 + me % 2
    rows[0] = up_ref[...]
    rows[1] = mid_ref[...]
    rows[2] = down_ref[...]
    lane = lax.broadcasted_iota(I32, (PAD, 128), 1)
    sources = ((own_ref, 0, q_own), (beside_ref, 0, q_own ^ 2), (across_ref, 432, q_own ^ 1), (opposite_ref, 0, q_own ^ 3))
    totals = [jnp.zeros((PAD, RANK), F32)] * 2
    for g in range(3):
        level = g // 2
        for which, (ref, start, q) in enumerate(sources):
            rest = jnp.zeros((PAD, 128), F32)
            for s in range(4):
                if 4 * g + s == SLOTS[0]:
                    stack[which, g, :, 128 * s : 128 * (s + 1)] = jnp.zeros((PAD, 128), BF16)
                    continue
                code = lists_ref[4 + q, s] if level else lists_ref[q, 4 * g + s]
                valid = code >= 0
                safe = jnp.where(valid, code, y * (8 if level else 16))
                row, col = (safe // 4, safe % 4) if level else (safe // 8, safe % 8)
                zh, place = (col, row % 2) if level else (col // 2, row % 2 * 2 + col % 2)
                plane = row // 2 - y + 1
                main = rows[plane, zh, 5 * level + place].astype(F32)
                stack[which, g, :, 128 * s : 128 * (s + 1)] = jnp.where(valid, main, 0.0).astype(BF16)
                turned = pltpu.roll(rows[plane, zh, 4 + 3 * level].astype(F32), (s + 4 - place) % 4 * 32, 1)
                inside = (lane >= 32 * s) & (lane < jnp.where(valid, 32 * (s + 1), 0))
                rest = jnp.where(inside, turned, rest)
            stack[which, g, :, 512:] = rest.astype(BF16)
            main = ref[start + RANK * g : start + RANK * (g + 1), :]
            last = ref[start + 3 * RANK : start + 4 * RANK, 128 * g : 128 * (g + 1)]
            totals[level] = totals[level] + mul_t(stack[which, g, :, :512], main) + mul_t(stack[which, g, :, 512:], last)
    wide[...] = jnp.zeros_like(wide)
    block = packed(totals[0], totals[1], jnp.zeros((8, 128), F32), wide)
    for d in range(8):
        out_ref[d] = block


def down_body(me_ref, got_ref, level_ref, one_ref, basis_ref, near_ref, out_ref, wide, local):
    me = me_ref[0]
    zl_own = me // 2 % 2
    for q in range(4):
        base = q // 2 * 4 + q % 2
        mine = got_ref[base + zl_own * 2].astype(F32)
        both = got_ref[base].astype(F32) + got_ref[base + 2].astype(F32)
        wide[:, :128] = both[PAD : 2 * PAD]
        wide[:, 128:] = rest_of(both, 1)
        second = wide[:, :RANK].astype(BF16)
        wide[:, :128] = mine[:PAD]
        wide[:, 128:] = rest_of(mine, 0)
        local[PAD * q : PAD * (q + 1), :] = wide[:, :RANK] + mul_t(second, level_ref[...])
    one = mul(spreader(4, 144, True), local[...].astype(BF16)).astype(BF16)
    leaf = mul_t(one, one_ref[...]).astype(BF16)
    out_ref[...] = (near_ref[...] + mul(leaf, basis_ref[...])).astype(BF16)


def slot_of(list_ref, me, apart):
    found = jnp.int32(0)
    for k in range(1, 4):
        found = jnp.where(list_ref[0, k] == me + apart, k, found)
    return found


def side_body(me_ref, list_ref, x_ref, blocks_ref, chip_ref, cross_ref, below_ref):
    me = me_ref[0]
    even = me % 2 == 0
    x = x_ref[...]
    chip_ref[0:144] = x
    cross_ref[0] = x
    right_one = mul(x, blocks_ref[slot_of(list_ref, me, 1)]).astype(BF16)
    right_two = mul(x, blocks_ref[slot_of(list_ref, me, 17)]).astype(BF16)
    left = mul(x, blocks_ref[slot_of(list_ref, me, 15)]).astype(BF16)
    below_ref[...] = mul(x, blocks_ref[slot_of(list_ref, me, 16)]).astype(BF16)

    @pl.when(even)
    def _():
        chip_ref[144:288] = right_one
        chip_ref[288:432] = right_two
        cross_ref[1] = left
        cross_ref[2] = jnp.zeros_like(left)

    @pl.when(jnp.logical_not(even))
    def _():
        cross_ref[1] = right_one
        cross_ref[2] = right_two
        chip_ref[144:288] = left
        chip_ref[288:432] = jnp.zeros_like(left)


def pack_body(one_ref, two_ref, own_ref, wide):
    wide[...] = jnp.zeros_like(wide)
    own_ref[3 * RANK :, 384:] = jnp.zeros((RANK, 128), BF16)
    for g in range(3):
        rest = jnp.zeros((RANK, 128), F32)
        for s in range(4):
            place = (slice(RANK * g, RANK * (g + 1)), slice(128 * s, 128 * (s + 1)))
            if 4 * g + s == SLOTS[0]:
                own_ref[place] = jnp.zeros((RANK, 128), BF16)
                continue
            block = one_ref[4 * g + s] if g < 2 else two_ref[s]
            own_ref[place] = block[:, :128]
            wide[:, :32] = block[:, 128:].astype(F32)
            rest += wide[...] if s == 0 else pltpu.roll(wide[...], 32 * s, 1)
        own_ref[3 * RANK :, 128 * g : 128 * (g + 1)] = rest.astype(BF16)


def turn_body(me_ref, x_ref, below_ref, chip_ref, cross_ref, rise_ref, sink_ref, mirror_ref):
    even = me_ref[0] % 2 == 0
    rise_ref[1] = x_ref[...]

    @pl.when(even)
    def _():
        rise_ref[0] = cross_ref[0]
        rise_ref[2] = chip_ref[0:144]
        mirror_ref[...] = cross_ref[1]
        sides = chip_ref[144:288].astype(F32) + cross_ref[2].astype(F32)
        sink_ref[...] = (below_ref[...].astype(F32) + sides).astype(BF16)

    @pl.when(jnp.logical_not(even))
    def _():
        rise_ref[0] = chip_ref[0:144]
        rise_ref[2] = cross_ref[0]
        mirror_ref[...] = chip_ref[144:288]
        sides = cross_ref[1].astype(F32) + chip_ref[288:432].astype(F32)
        sink_ref[...] = (below_ref[...].astype(F32) + sides).astype(BF16)


def near_body(me_ref, list_ref, self_ref, blocks_ref, rise_ref, mirror_ref, risen_ref, sunk_ref, out_ref):
    me = me_ref[0]
    total = mul_t(rise_ref[1], self_ref[...])
    total += mul_t(rise_ref[2], blocks_ref[slot_of(list_ref, me, 1)])
    total += mul_t(risen_ref[0], blocks_ref[slot_of(list_ref, me, 15)])
    total += mul_t(risen_ref[1], blocks_ref[slot_of(list_ref, me, 16)])
    total += mul_t(risen_ref[2], blocks_ref[slot_of(list_ref, me, 17)])
    out_ref[...] = total + mirror_ref[...].astype(F32) + sunk_ref[...].astype(F32)


def shards(
    right_sides,
    near_self,
    near_blocks,
    near_list,
    basis,
    transfer_one,
    transfer_two,
    couple_one,
    couple_two,
    far_list_one,
    far_list_two,
):
    me = lax.axis_index(AXES).astype(I32).reshape(1)
    x = right_sides[0, 0].T
    vectors = basis[0, 0].T
    one = transfer_one[0, 0]
    blocks = near_blocks[0, 0]
    links = near_list[0]

    across_gy = ("zh", "zl", "c")
    along_gx = ("y", "xh", "xl")
    swap = [(0, 1), (1, 0)]

    message, own, chip, cross, below = fused(
        Stage(
            up_body,
            [shape(16, ROWS, 128)],
            [pltpu.VMEM((2, PAD, 256), F32)],
            [x, vectors, one, transfer_two[0, 0]],
            lists=[far_list_one[0], far_list_two[0]],
            repeats={0: [d // 4 % 2 * 2 + d % 2 for d in range(16)]},
        ),
        Stage(
            pack_body,
            [shape(4 * RANK, 512)],
            [pltpu.VMEM((RANK, 128), F32)],
            [couple_one[0, 0], couple_two[0, 0]],
            also=[(0, 2, 432)],
        ),
        Stage(
            side_body,
            [shape(1072, 512), shape(3, 144, 512), shape(144, 512)],
            [],
            [x, blocks],
            lists=[links],
            scalars=[me],
            heads={0: 432},
        ),
        flops=4 * 10**8,
    )
    got = lax.all_to_all(message, ("xh", "xl", "zl", "c"), 0, 0)
    from_chip = lax.ppermute(chip, "c", swap)
    steps = [(i, i + 1) for i in range(1, 15, 2)] + [(i, i - 1) for i in range(2, 16, 2)]
    from_cross = lax.ppermute(cross, across_gy, steps)
    beside = lax.ppermute(own, "xl", swap)
    window, level, codes = fused(
        Stage(
            merge_body,
            [shape(4, SLABS, PAD, 128), shape(RANK, RANK), shape(8, 128, dtype=I32)],
            [pltpu.VMEM((PAD, 256), F32), pltpu.VMEM((4, RANK, 256), F32)],
            [got],
            scalars=[me],
            repeats={0: [0] * 4},
        ),
        flops=6 * 10**9,
    )
    plane = lax.all_to_all(window, "zh", 0, 0)
    below, _ = lax.optimization_barrier((below, window))
    rise, sink, mirror = fused(
        Stage(
            turn_body, [shape(3, 144, 512), shape(144, 512), shape(144, 512)], [], [x, below, from_chip, from_cross], scalars=[me]
        )
    )
    risen = lax.ppermute(rise, along_gx, [(i + 1, i) for i in range(31)])
    sunk = lax.ppermute(sink, along_gx, [(i, i + 1) for i in range(31)])
    beside, _ = lax.optimization_barrier((beside, window))
    opposite = lax.ppermute(beside, "c", swap)
    above = lax.ppermute(plane, "y", [(i, i + 1) for i in range(7)])
    under = lax.ppermute(plane, "y", [(i + 1, i) for i in range(7)])
    near = call(
        near_body, shape(144, 512, dtype=F32), [], [SMEM, SMEM] + [VMEM] * 6, 5 * 10**9, 4 * 10**6
    )(me, links, near_self[0, 0], blocks, rise, mirror, risen, sunk)
    codes = after(codes, near)
    partial = call(
        couple_body,
        shape(8, ROWS, 128),
        [
            pltpu.VMEM((3, 4, SLABS, PAD, 128), BF16),
            pltpu.VMEM((4, 3, PAD, 640), BF16),
            pltpu.VMEM((2, PAD, 256), F32),
        ],
        [SMEM, SMEM] + [VMEM] * 7,
        6 * 10**8,
        4 * 10**6,
    )(me, codes, above, plane, under, own, beside, from_chip, opposite)
    sums = lax.all_to_all(partial, ("xl", "zl", "c"), 0, 0)
    applied = call(
        down_body,
        shape(144, 512),
        [pltpu.VMEM((PAD, 256), F32), pltpu.VMEM((RANK, RANK), F32)],
        [SMEM] + [VMEM] * 5,
        10**8,
        10**6,
    )(me, sums, level, one, vectors, near)
    return applied.T[None, None]


def solution(mesh):
    split = Mesh(mesh.devices.reshape(8, 2, 2, 4, 2, 2), AXES)
    rows, cols = AXES[:3], AXES[3:]

    def spec(rank):
        return P(rows, cols, *[None] * (rank - 2))

    ranks = (4, 4, 5, 3, 4, 4, 4, 5, 5, 3, 3)
    return jax.shard_map(
        shards, mesh=split, in_specs=tuple(map(spec, ranks)), out_specs=spec(4), check_vma=False
    )
```

```python
import functools

import jax
import jax.numpy as jnp
from jax import lax
from jax.experimental import pallas as pl
from jax.experimental.pallas import tpu as pltpu
from jax.sharding import Mesh, PartitionSpec as P

AXES = ("y", "xh", "xl", "zh", "zl", "c")
F32, BF16, I32 = jnp.float32, jnp.bfloat16, jnp.int32
RANK, CHUNK, PAD = 160, 36, 40
SLOTS = (7, 4)
VMEM = pl.BlockSpec(memory_space=pltpu.VMEM)
SMEM = pl.BlockSpec(memory_space=pltpu.SMEM)
ANY = pl.BlockSpec(memory_space=pl.ANY)
SLABS = 8


class Stage:
    def __init__(self, body, outs, scratch, args, lists=(), scalars=(), repeats=None, heads=None, also=(), direct=()):
        self.body, self.outs, self.scratch, self.args = body, outs, scratch, list(args)
        self.lists, self.scalars, self.repeats = list(lists), list(scalars), repeats or {}
        self.heads, self.also, self.direct = heads or {}, also, list(direct)
        self.ready = [
            shape(max(self.repeats[o]) + 1, *out.shape[1:], dtype=out.dtype)
            if o in self.repeats
            else shape(self.heads.get(o, out.shape[0]), *out.shape[1:], dtype=out.dtype)
            for o, out in enumerate(outs)
        ]


def fused(*stages, flops=10**8, limit=60):
    shared = []

    def index(array):
        for i, held in enumerate(shared):
            if held is array:
                return i
        shared.append(array)
        return len(shared) - 1

    uses = [[index(a) for a in stage.args] for stage in stages]
    lists = [a for stage in stages for a in stage.lists]
    scalars = [a for stage in stages for a in stage.scalars]
    directs = [a for stage in stages for a in stage.direct]
    outs = [o for stage in stages for o in stage.outs]
    ready = [o for stage in stages for o in stage.ready]
    n_copies = sum(len(stage.repeats.get(o, (0,))) for stage in stages for o in range(len(stage.outs)))
    n_copies += sum(len(stage.also) for stage in stages)

    def run(*refs):
        refs = list(refs)

        def take(n):
            taken = refs[:n]
            del refs[:n]
            return taken

        ins, tables, plain = take(len(shared)), take(len(lists)), take(len(scalars))
        whole_ins, results = take(len(directs)), take(len(outs))
        held, read, buffers, in_sems, out_sems = take(len(shared)), take(len(lists)), take(len(outs)), *take(2)
        fetch = [
            pltpu.make_async_copy(source, target, in_sems.at[i])
            for i, (source, target) in enumerate(zip(ins + tables, held + read))
        ]
        for copy in fetch:
            copy.start()
        for copy in fetch[len(shared) :]:
            copy.wait()
        arrived, leaving, everything = set(), [], list(results)
        for stage, use in zip(stages, uses):
            for i in use:
                if i not in arrived:
                    fetch[i].wait()
                    arrived.add(i)
            mine = [buffers.pop(0) for _ in stage.outs]
            targets = [results.pop(0) for _ in stage.outs]
            heads = [plain.pop(0) for _ in stage.scalars] + [read.pop(0) for _ in stage.lists]
            given = [held[i] for i in use] + [whole_ins.pop(0) for _ in stage.direct]
            stage.body(*heads, *given, *mine, *take(len(stage.scratch)))
            for o in range(len(stage.outs)):
                whole = targets[o].at[pl.ds(0, stage.heads[o])] if o in stage.heads else targets[o]
                pairs = [(mine[o], whole)]
                if o in stage.repeats:
                    pairs = [(mine[o].at[part], targets[o].at[d]) for d, part in enumerate(stage.repeats[o])]
                for held_at, out, row in stage.also:
                    if held_at == o:
                        pairs.append((mine[o], everything[out].at[pl.ds(row, mine[o].shape[0])]))
                for source, target in pairs:
                    leaving.append(pltpu.make_async_copy(source, target, out_sems.at[len(leaving)]))
                    leaving[-1].start()
        for copy in leaving:
            copy.wait()

    buffers = [pltpu.VMEM(a.shape, a.dtype) for a in shared]
    buffers += [pltpu.SMEM(a.shape, a.dtype) for a in lists]
    buffers += [pltpu.VMEM(a.shape, a.dtype) for a in ready]
    buffers += [pltpu.SemaphoreType.DMA((len(shared) + len(lists),)), pltpu.SemaphoreType.DMA((n_copies,))]
    moved = sum(a.size * a.dtype.itemsize for a in [*shared, *outs])
    return pl.pallas_call(
        run,
        out_shape=outs,
        in_specs=[ANY] * (len(shared) + len(lists)) + [SMEM] * len(scalars) + [VMEM] * len(directs),
        out_specs=[ANY] * len(outs),
        scratch_shapes=buffers + [b for stage in stages for b in stage.scratch],
        compiler_params=pltpu.CompilerParams(vmem_limit_bytes=limit * 2**20),
        cost_estimate=pl.CostEstimate(flops=flops, bytes_accessed=moved, transcendentals=0),
    )(*shared, *lists, *scalars, *directs)


def call(body, outs, scratch, specs, flops, moved):
    return pl.pallas_call(
        body,
        out_shape=outs,
        in_specs=specs,
        out_specs=jax.tree.map(lambda _: VMEM, outs),
        scratch_shapes=scratch,
        compiler_params=pltpu.CompilerParams(vmem_limit_bytes=16 * 2**20),
        cost_estimate=pl.CostEstimate(flops=flops, bytes_accessed=moved, transcendentals=0),
    )


def after(value, *others):
    return lax.optimization_barrier((value, *others))[0]


def shape(*dims, dtype=BF16):
    return jax.ShapeDtypeStruct(dims, dtype)


def mul(a, b):
    return lax.dot_general(a, b, (((1,), (0,)), ((), ())), preferred_element_type=F32)


def mul_t(a, b):
    return lax.dot_general(a, b, (((1,), (1,)), ((), ())), preferred_element_type=F32)


def spreader(groups, cols, transposed=False):
    dims = (cols, groups * PAD) if transposed else (groups * PAD, cols)
    padded = lax.broadcasted_iota(I32, dims, 1 if transposed else 0)
    dense = lax.broadcasted_iota(I32, dims, 0 if transposed else 1)
    hit = jnp.zeros(dims, jnp.bool_)
    for g in range(groups):
        inside = (padded >= PAD * g) & (padded < PAD * g + CHUNK)
        hit = hit | (inside & (dense == padded - (PAD - CHUNK) * g))
    return jnp.where(hit, 1.0, 0.0).astype(BF16)


ROWS = 112


def packed(a, b, tail, wide):
    wide[0, :, :RANK] = a
    wide[1, :, :RANK] = b
    first, second = wide[0, :, 128:], wide[1, :, 128:]
    rest = (
        first[:24]
        + pltpu.roll(jnp.concatenate([first[24:], tail], axis=0), 32, 1)
        + pltpu.roll(second[:24], 64, 1)
        + pltpu.roll(jnp.concatenate([second[24:], jnp.zeros((8, 128), F32)], axis=0), 96, 1)
    )
    return jnp.concatenate([wide[0, :, :128], wide[1, :, :128], rest, jnp.zeros((8, 128), F32)], axis=0).astype(BF16)


def rest_of(block, which):
    rest = block[2 * PAD : 2 * PAD + 24]
    left = pltpu.roll(rest, 64, 1) if which else rest
    return jnp.concatenate([left, pltpu.roll(left, 96, 1)[:16]], axis=0)


def up_body(far_one_ref, far_two_ref, x_ref, basis_ref, one_ref, two_ref, out_ref, wide):
    wide[...] = jnp.zeros_like(wide)
    row = lax.broadcasted_iota(I32, (8, 128), 0)
    lane = lax.broadcasted_iota(I32, (8, 128), 1)
    tail = jnp.full((8, 128), -1.0, F32)
    for r, ref in enumerate((far_one_ref, far_two_ref)):
        for k in range(SLOTS[r]):
            tail = jnp.where((row == r) & (lane == k), ref[0, k].astype(F32), tail)
    tail = jnp.where(lane < 32, tail, 0.0)
    leaf = mul_t(x_ref[...], basis_ref[...]).astype(BF16)
    up = mul(leaf, one_ref[...]).astype(BF16)
    chunks = mul(spreader(4, 144), up)
    quarter = two_ref[...].astype(F32)
    for q in range(4):
        out_ref[q] = packed(chunks[PAD * q : PAD * (q + 1)], quarter, tail, wide)


def merge_body(me_ref, got_ref, window_ref, level_ref, lists_ref, wide, levels):
    me = me_ref[0]
    own = (me // 32) % 2 * 2 + me // 2 % 2
    lane = lax.broadcasted_iota(I32, (PAD, 128), 1)
    rests = [jnp.zeros((PAD, 128), F32)] * 2
    slabs = [None] * SLABS

    def deposit(level, place, main, rest):
        slabs[5 * level + place] = main
        rest = jnp.where(lane < 32, rest, 0.0)
        rests[level] = rests[level] + (pltpu.roll(rest, 32 * place, 1) if place else rest)

    for xh in range(2):
        second = jnp.zeros((PAD, RANK), F32)
        for zl in range(2):
            total = jnp.zeros((ROWS, 128), F32)
            for q in range(4):
                block = got_ref[xh * 8 + (q // 2) * 4 + zl * 2 + q % 2].astype(F32)
                total += block
                rows = slice(PAD * q, PAD * (q + 1))
                levels[xh * 2 + zl, rows, :128] = block[PAD : 2 * PAD]
                levels[xh * 2 + zl, rows, 128:] = rest_of(block, 1)
            main, rest = total[:PAD], rest_of(total, 0)
            wide[:, :128] = main
            wide[:, 128:] = rest
            first = wide[:, :RANK]
            deposit(0, xh * 2 + zl, main, rest)
            second += mul(first.astype(BF16), levels[xh * 2 + zl, :, :RANK].astype(BF16))
        wide[:, :RANK] = second
        deposit(1, xh, wide[:, :128], wide[:, 128:])
    slabs[4], slabs[7] = rests
    window_ref[0] = jnp.concatenate(slabs, axis=0).astype(BF16)
    level_ref[...] = levels[own, :, :RANK].astype(BF16)
    for q in range(4):
        place = (me // 32) % 2 * 8 + (q // 2) * 4 + me // 2 % 2 * 2 + q % 2
        tail = pltpu.roll(got_ref[place].astype(F32)[2 * PAD : 2 * PAD + 24], 96, 1)
        lists_ref[q : q + 1, :] = tail[16:17].astype(I32)
        lists_ref[4 + q : 5 + q, :] = tail[17:18].astype(I32)


def couple_body(me_ref, lists_ref, up_ref, mid_ref, down_ref, own_ref, beside_ref, across_ref, opposite_ref, out_ref, rows, stack, wide):
    me = me_ref[0]
    y = me // 64
    q_own = me // 16 % 2 * 2 + me % 2
    for p, ref in enumerate((up_ref, mid_ref, down_ref)):
        for zh in range(4):
            block = ref[zh].astype(F32)
            for g in range(SLABS):
                rows[p, zh, g] = block[PAD * g : PAD * (g + 1)]
    lane = lax.broadcasted_iota(I32, (PAD, 128), 1)
    sources = ((own_ref, 0, q_own), (beside_ref, 0, q_own ^ 2), (across_ref, 432, q_own ^ 1), (opposite_ref, 0, q_own ^ 3))
    totals = [jnp.zeros((PAD, RANK), F32)] * 2
    for g in range(3):
        level = g // 2
        for which, (ref, start, q) in enumerate(sources):
            rest = jnp.zeros((PAD, 128), F32)
            for s in range(4):
                if 4 * g + s == SLOTS[0]:
                    stack[which, g, :, 128 * s : 128 * (s + 1)] = jnp.zeros((PAD, 128), BF16)
                    continue
                code = lists_ref[4 + q, s] if level else lists_ref[q, 4 * g + s]
                valid = code >= 0
                safe = jnp.where(valid, code, y * (8 if level else 16))
                row, col = (safe // 4, safe % 4) if level else (safe // 8, safe % 8)
                zh, place = (col, row % 2) if level else (col // 2, row % 2 * 2 + col % 2)
                plane = row // 2 - y + 1
                main = rows[plane, zh, 5 * level + place]
                stack[which, g, :, 128 * s : 128 * (s + 1)] = jnp.where(valid, main, 0.0).astype(BF16)
                turned = pltpu.roll(rows[plane, zh, 4 + 3 * level], (s + 4 - place) % 4 * 32, 1)
                inside = (lane >= 32 * s) & (lane < jnp.where(valid, 32 * (s + 1), 0))
                rest = jnp.where(inside, turned, rest)
            stack[which, g, :, 512:] = rest.astype(BF16)
            main = ref[start + RANK * g : start + RANK * (g + 1), :]
            last = ref[start + 3 * RANK : start + 4 * RANK, 128 * g : 128 * (g + 1)]
            totals[level] = totals[level] + mul_t(stack[which, g, :, :512], main) + mul_t(stack[which, g, :, 512:], last)
    wide[...] = jnp.zeros_like(wide)
    block = packed(totals[0], totals[1], jnp.zeros((8, 128), F32), wide)
    for d in range(8):
        out_ref[d] = block


def down_body(me_ref, got_ref, level_ref, one_ref, basis_ref, near_ref, out_ref, wide, local):
    me = me_ref[0]
    zl_own = me // 2 % 2
    for q in range(4):
        base = q // 2 * 4 + q % 2
        mine = got_ref[base + zl_own * 2].astype(F32)
        both = got_ref[base].astype(F32) + got_ref[base + 2].astype(F32)
        wide[:, :128] = both[PAD : 2 * PAD]
        wide[:, 128:] = rest_of(both, 1)
        second = wide[:, :RANK].astype(BF16)
        wide[:, :128] = mine[:PAD]
        wide[:, 128:] = rest_of(mine, 0)
        local[PAD * q : PAD * (q + 1), :] = wide[:, :RANK] + mul_t(second, level_ref[...])
    one = mul(spreader(4, 144, True), local[...].astype(BF16)).astype(BF16)
    leaf = mul_t(one, one_ref[...]).astype(BF16)
    out_ref[...] = (near_ref[...] + mul(leaf, basis_ref[...])).astype(BF16)


def slot_of(list_ref, me, apart):
    found = jnp.int32(0)
    for k in range(1, 4):
        found = jnp.where(list_ref[0, k] == me + apart, k, found)
    return found


def side_body(me_ref, list_ref, x_ref, blocks_ref, chip_ref, cross_ref, below_ref):
    me = me_ref[0]
    even = me % 2 == 0
    x = x_ref[...]
    chip_ref[0:144] = x
    cross_ref[0] = x
    right_one = mul(x, blocks_ref[slot_of(list_ref, me, 1)]).astype(BF16)
    right_two = mul(x, blocks_ref[slot_of(list_ref, me, 17)]).astype(BF16)
    left = mul(x, blocks_ref[slot_of(list_ref, me, 15)]).astype(BF16)
    below_ref[...] = mul(x, blocks_ref[slot_of(list_ref, me, 16)]).astype(BF16)

    @pl.when(even)
    def _():
        chip_ref[144:288] = right_one
        chip_ref[288:432] = right_two
        cross_ref[1] = left
        cross_ref[2] = jnp.zeros_like(left)

    @pl.when(jnp.logical_not(even))
    def _():
        cross_ref[1] = right_one
        cross_ref[2] = right_two
        chip_ref[144:288] = left
        chip_ref[288:432] = jnp.zeros_like(left)


def pack_body(one_ref, two_ref, own_ref, wide):
    wide[...] = jnp.zeros_like(wide)
    own_ref[3 * RANK :, 384:] = jnp.zeros((RANK, 128), BF16)
    for g in range(3):
        rest = jnp.zeros((RANK, 128), F32)
        for s in range(4):
            place = (slice(RANK * g, RANK * (g + 1)), slice(128 * s, 128 * (s + 1)))
            if 4 * g + s == SLOTS[0]:
                own_ref[place] = jnp.zeros((RANK, 128), BF16)
                continue
            block = one_ref[4 * g + s] if g < 2 else two_ref[s]
            own_ref[place] = block[:, :128]
            wide[:, :32] = block[:, 128:].astype(F32)
            rest += wide[...] if s == 0 else pltpu.roll(wide[...], 32 * s, 1)
        own_ref[3 * RANK :, 128 * g : 128 * (g + 1)] = rest.astype(BF16)


def turn_body(me_ref, x_ref, below_ref, chip_ref, cross_ref, rise_ref, sink_ref, mirror_ref):
    even = me_ref[0] % 2 == 0
    rise_ref[1] = x_ref[...]

    @pl.when(even)
    def _():
        rise_ref[0] = cross_ref[0]
        rise_ref[2] = chip_ref[0:144]
        mirror_ref[...] = cross_ref[1]
        sides = chip_ref[144:288].astype(F32) + cross_ref[2].astype(F32)
        sink_ref[...] = (below_ref[...].astype(F32) + sides).astype(BF16)

    @pl.when(jnp.logical_not(even))
    def _():
        rise_ref[0] = chip_ref[0:144]
        rise_ref[2] = cross_ref[0]
        mirror_ref[...] = chip_ref[144:288]
        sides = cross_ref[1].astype(F32) + chip_ref[288:432].astype(F32)
        sink_ref[...] = (below_ref[...].astype(F32) + sides).astype(BF16)


def near_body(me_ref, list_ref, self_ref, blocks_ref, rise_ref, mirror_ref, risen_ref, sunk_ref, out_ref):
    me = me_ref[0]
    total = mul_t(rise_ref[1], self_ref[...])
    total += mul_t(rise_ref[2], blocks_ref[slot_of(list_ref, me, 1)])
    total += mul_t(risen_ref[0], blocks_ref[slot_of(list_ref, me, 15)])
    total += mul_t(risen_ref[1], blocks_ref[slot_of(list_ref, me, 16)])
    total += mul_t(risen_ref[2], blocks_ref[slot_of(list_ref, me, 17)])
    out_ref[...] = total + mirror_ref[...].astype(F32) + sunk_ref[...].astype(F32)


def shards(
    right_sides,
    near_self,
    near_blocks,
    near_list,
    basis,
    transfer_one,
    transfer_two,
    couple_one,
    couple_two,
    far_list_one,
    far_list_two,
):
    me = lax.axis_index(AXES).astype(I32).reshape(1)
    x = right_sides[0, 0].T
    vectors = basis[0, 0].T
    one = transfer_one[0, 0]
    blocks = near_blocks[0, 0]
    links = near_list[0]

    across_gy = ("zh", "zl", "c")
    along_gx = ("y", "xh", "xl")
    swap = [(0, 1), (1, 0)]

    message, own, chip, cross, below = fused(
        Stage(
            up_body,
            [shape(16, ROWS, 128)],
            [pltpu.VMEM((2, PAD, 256), F32)],
            [x, vectors, one],
            direct=[transfer_two[0, 0]],
            lists=[far_list_one[0], far_list_two[0]],
            repeats={0: [d // 4 % 2 * 2 + d % 2 for d in range(16)]},
        ),
        Stage(
            pack_body,
            [shape(4 * RANK, 512)],
            [pltpu.VMEM((RANK, 128), F32)],
            [couple_one[0, 0], couple_two[0, 0]],
            also=[(0, 2, 432)],
        ),
        Stage(
            side_body,
            [shape(1072, 512), shape(3, 144, 512), shape(144, 512)],
            [],
            [x, blocks],
            lists=[links],
            scalars=[me],
            heads={0: 432},
        ),
        flops=4 * 10**8,
    )
    got = lax.all_to_all(message, ("xh", "xl", "zl", "c"), 0, 0)
    from_chip = lax.ppermute(chip, "c", swap)
    steps = [(i, i + 1) for i in range(1, 15, 2)] + [(i, i - 1) for i in range(2, 16, 2)]
    from_cross = lax.ppermute(cross, across_gy, steps)
    beside = lax.ppermute(own, "xl", swap)
    window, level, codes = fused(
        Stage(
            merge_body,
            [shape(4, SLABS * PAD, 128), shape(RANK, RANK), shape(8, 128, dtype=I32)],
            [pltpu.VMEM((PAD, 256), F32), pltpu.VMEM((4, RANK, 256), F32)],
            [got],
            scalars=[me],
            repeats={0: [0] * 4},
        ),
        flops=6 * 10**9,
    )
    plane = lax.all_to_all(window, "zh", 0, 0)
    below, _ = lax.optimization_barrier((below, window))
    rise, sink, mirror = fused(
        Stage(
            turn_body, [shape(3, 144, 512), shape(144, 512), shape(144, 512)], [], [x, below, from_chip, from_cross], scalars=[me]
        )
    )
    risen = lax.ppermute(rise, along_gx, [(i + 1, i) for i in range(31)])
    sunk = lax.ppermute(sink, along_gx, [(i, i + 1) for i in range(31)])
    beside, _ = lax.optimization_barrier((beside, window))
    opposite = lax.ppermute(beside, "c", swap)
    above = lax.ppermute(plane, "y", [(i, i + 1) for i in range(7)])
    under = lax.ppermute(plane, "y", [(i + 1, i) for i in range(7)])
    near = call(
        near_body, shape(144, 512, dtype=F32), [], [SMEM, SMEM] + [VMEM] * 6, 5 * 10**9, 4 * 10**6
    )(me, links, near_self[0, 0], blocks, rise, mirror, risen, sunk)
    codes = after(codes, near)
    partial = call(
        couple_body,
        shape(8, ROWS, 128),
        [
            pltpu.VMEM((3, 4, SLABS, PAD, 128), F32),
            pltpu.VMEM((4, 3, PAD, 640), BF16),
            pltpu.VMEM((2, PAD, 256), F32),
        ],
        [SMEM, SMEM] + [VMEM] * 7,
        6 * 10**8,
        4 * 10**6,
    )(me, codes, above, plane, under, own, beside, from_chip, opposite)
    sums = lax.all_to_all(partial, ("xl", "zl", "c"), 0, 0)
    applied = call(
        down_body,
        shape(144, 512),
        [pltpu.VMEM((PAD, 256), F32), pltpu.VMEM((RANK, RANK), F32)],
        [SMEM] + [VMEM] * 5,
        10**8,
        10**6,
    )(me, sums, level, one, vectors, near)
    return applied.T[None, None]


def solution(mesh):
    split = Mesh(mesh.devices.reshape(8, 2, 2, 4, 2, 2), AXES)
    rows, cols = AXES[:3], AXES[3:]

    def spec(rank):
        return P(rows, cols, *[None] * (rank - 2))

    ranks = (4, 4, 5, 3, 4, 4, 4, 5, 5, 3, 3)
    return jax.shard_map(
        shards, mesh=split, in_specs=tuple(map(spec, ranks)), out_specs=spec(4), check_vma=False
    )
```

```python
import functools

import jax
import jax.numpy as jnp
from jax import lax
from jax.experimental import pallas as pl
from jax.experimental.pallas import tpu as pltpu
from jax.sharding import Mesh, PartitionSpec as P

AXES = ("y", "xh", "xl", "zh", "zl", "c")
F32, BF16, I32 = jnp.float32, jnp.bfloat16, jnp.int32
RANK, CHUNK, PAD = 160, 36, 40
SLOTS = (7, 4)
VMEM = pl.BlockSpec(memory_space=pltpu.VMEM)
SMEM = pl.BlockSpec(memory_space=pltpu.SMEM)
ANY = pl.BlockSpec(memory_space=pl.ANY)
SLABS = 8


class Stage:
    def __init__(self, body, outs, scratch, args, lists=(), scalars=(), repeats=None, heads=None, also=(), direct=(), first_rows=None):
        self.body, self.outs, self.scratch, self.args = body, outs, scratch, list(args)
        self.lists, self.scalars, self.repeats = list(lists), list(scalars), repeats or {}
        self.heads, self.also, self.direct = heads or {}, also, list(direct)
        self.first_rows = first_rows or {}
        self.ready = [
            shape(max(self.repeats[o]) + 1, *out.shape[1:], dtype=out.dtype)
            if o in self.repeats
            else shape(self.heads.get(o, out.shape[0]), *out.shape[1:], dtype=out.dtype)
            for o, out in enumerate(outs)
        ]


def fused(*stages, flops=10**8, limit=60):
    shared = []

    def index(array):
        for i, held in enumerate(shared):
            if held is array:
                return i
        shared.append(array)
        return len(shared) - 1

    uses = [[index(a) for a in stage.args] for stage in stages]
    fetched = {use[i]: n for stage, use in zip(stages, uses) for i, n in stage.first_rows.items()}
    lists = [a for stage in stages for a in stage.lists]
    scalars = [a for stage in stages for a in stage.scalars]
    directs = [a for stage in stages for a in stage.direct]
    outs = [o for stage in stages for o in stage.outs]
    ready = [o for stage in stages for o in stage.ready]
    n_copies = sum(len(stage.repeats.get(o, (0,))) for stage in stages for o in range(len(stage.outs)))
    n_copies += sum(len(stage.also) for stage in stages)

    def run(*refs):
        refs = list(refs)

        def take(n):
            taken = refs[:n]
            del refs[:n]
            return taken

        ins, tables, plain = take(len(shared)), take(len(lists)), take(len(scalars))
        whole_ins, results = take(len(directs)), take(len(outs))
        held, read, buffers, in_sems, out_sems = take(len(shared)), take(len(lists)), take(len(outs)), *take(2)
        parts = [ref.at[pl.ds(0, fetched[i])] if i in fetched else ref for i, ref in enumerate(ins)]
        fetch = [
            pltpu.make_async_copy(source, target, in_sems.at[i])
            for i, (source, target) in enumerate(zip(parts + tables, held + read))
        ]
        for copy in fetch:
            copy.start()
        for copy in fetch[len(shared) :]:
            copy.wait()
        arrived, leaving, everything = set(), [], list(results)
        for stage, use in zip(stages, uses):
            for i in use:
                if i not in arrived:
                    fetch[i].wait()
                    arrived.add(i)
            mine = [buffers.pop(0) for _ in stage.outs]
            targets = [results.pop(0) for _ in stage.outs]
            heads = [plain.pop(0) for _ in stage.scalars] + [read.pop(0) for _ in stage.lists]
            given = [held[i] for i in use] + [whole_ins.pop(0) for _ in stage.direct]
            stage.body(*heads, *given, *mine, *take(len(stage.scratch)))
            for o in range(len(stage.outs)):
                whole = targets[o].at[pl.ds(0, stage.heads[o])] if o in stage.heads else targets[o]
                pairs = [(mine[o], whole)]
                if o in stage.repeats:
                    pairs = [(mine[o].at[part], targets[o].at[d]) for d, part in enumerate(stage.repeats[o])]
                for held_at, out, row in stage.also:
                    if held_at == o:
                        pairs.append((mine[o], everything[out].at[pl.ds(row, mine[o].shape[0])]))
                for source, target in pairs:
                    leaving.append(pltpu.make_async_copy(source, target, out_sems.at[len(leaving)]))
                    leaving[-1].start()
        for copy in leaving:
            copy.wait()

    buffers = [pltpu.VMEM((fetched.get(i, a.shape[0]), *a.shape[1:]), a.dtype) for i, a in enumerate(shared)]
    buffers += [pltpu.SMEM(a.shape, a.dtype) for a in lists]
    buffers += [pltpu.VMEM(a.shape, a.dtype) for a in ready]
    buffers += [pltpu.SemaphoreType.DMA((len(shared) + len(lists),)), pltpu.SemaphoreType.DMA((n_copies,))]
    moved = sum(a.size * a.dtype.itemsize for a in [*shared, *outs])
    return pl.pallas_call(
        run,
        out_shape=outs,
        in_specs=[ANY] * (len(shared) + len(lists)) + [SMEM] * len(scalars) + [VMEM] * len(directs),
        out_specs=[ANY] * len(outs),
        scratch_shapes=buffers + [b for stage in stages for b in stage.scratch],
        compiler_params=pltpu.CompilerParams(vmem_limit_bytes=limit * 2**20),
        cost_estimate=pl.CostEstimate(flops=flops, bytes_accessed=moved, transcendentals=0),
    )(*shared, *lists, *scalars, *directs)


def call(body, outs, scratch, specs, flops, moved):
    return pl.pallas_call(
        body,
        out_shape=outs,
        in_specs=specs,
        out_specs=jax.tree.map(lambda _: VMEM, outs),
        scratch_shapes=scratch,
        compiler_params=pltpu.CompilerParams(vmem_limit_bytes=16 * 2**20),
        cost_estimate=pl.CostEstimate(flops=flops, bytes_accessed=moved, transcendentals=0),
    )


def after(value, *others):
    return lax.optimization_barrier((value, *others))[0]


def shape(*dims, dtype=BF16):
    return jax.ShapeDtypeStruct(dims, dtype)


def mul(a, b):
    return lax.dot_general(a, b, (((1,), (0,)), ((), ())), preferred_element_type=F32)


def mul_t(a, b):
    return lax.dot_general(a, b, (((1,), (1,)), ((), ())), preferred_element_type=F32)


def spreader(groups, cols, transposed=False):
    dims = (cols, groups * PAD) if transposed else (groups * PAD, cols)
    padded = lax.broadcasted_iota(I32, dims, 1 if transposed else 0)
    dense = lax.broadcasted_iota(I32, dims, 0 if transposed else 1)
    hit = jnp.zeros(dims, jnp.bool_)
    for g in range(groups):
        inside = (padded >= PAD * g) & (padded < PAD * g + CHUNK)
        hit = hit | (inside & (dense == padded - (PAD - CHUNK) * g))
    return jnp.where(hit, 1.0, 0.0).astype(BF16)


ROWS = 112


def packed(a, b, tail, wide):
    wide[0, :, :RANK] = a
    wide[1, :, :RANK] = b
    first, second = wide[0, :, 128:], wide[1, :, 128:]
    rest = (
        first[:24]
        + pltpu.roll(jnp.concatenate([first[24:], tail], axis=0), 32, 1)
        + pltpu.roll(second[:24], 64, 1)
        + pltpu.roll(jnp.concatenate([second[24:], jnp.zeros((8, 128), F32)], axis=0), 96, 1)
    )
    return jnp.concatenate([wide[0, :, :128], wide[1, :, :128], rest, jnp.zeros((8, 128), F32)], axis=0).astype(BF16)


def rest_of(block, which):
    rest = block[2 * PAD : 2 * PAD + 24]
    left = pltpu.roll(rest, 64, 1) if which else rest
    return jnp.concatenate([left, pltpu.roll(left, 96, 1)[:16]], axis=0)


def up_body(far_one_ref, far_two_ref, x_ref, basis_ref, one_ref, two_ref, out_ref, wide):
    wide[...] = jnp.zeros_like(wide)
    row = lax.broadcasted_iota(I32, (8, 128), 0)
    lane = lax.broadcasted_iota(I32, (8, 128), 1)
    tail = jnp.full((8, 128), -1.0, F32)
    for r, ref in enumerate((far_one_ref, far_two_ref)):
        for k in range(SLOTS[r]):
            tail = jnp.where((row == r) & (lane == k), ref[0, k].astype(F32), tail)
    tail = jnp.where(lane < 32, tail, 0.0)
    leaf = mul_t(x_ref[...], basis_ref[...]).astype(BF16)
    up = mul(leaf, one_ref[...]).astype(BF16)
    chunks = mul(spreader(4, 144), up)
    quarter = two_ref[...].astype(F32)
    for q in range(4):
        out_ref[q] = packed(chunks[PAD * q : PAD * (q + 1)], quarter, tail, wide)


def merge_body(me_ref, got_ref, window_ref, level_ref, lists_ref, wide, levels):
    me = me_ref[0]
    own = (me // 32) % 2 * 2 + me // 2 % 2
    lane = lax.broadcasted_iota(I32, (PAD, 128), 1)
    rests = [jnp.zeros((PAD, 128), F32)] * 2
    slabs = [None] * SLABS

    def deposit(level, place, main, rest):
        slabs[5 * level + place] = main
        rest = jnp.where(lane < 32, rest, 0.0)
        rests[level] = rests[level] + (pltpu.roll(rest, 32 * place, 1) if place else rest)

    for xh in range(2):
        second = jnp.zeros((PAD, RANK), F32)
        for zl in range(2):
            total = jnp.zeros((ROWS, 128), F32)
            for q in range(4):
                block = got_ref[xh * 8 + (q // 2) * 4 + zl * 2 + q % 2].astype(F32)
                total += block
                rows = slice(PAD * q, PAD * (q + 1))
                levels[xh * 2 + zl, rows, :128] = block[PAD : 2 * PAD]
                levels[xh * 2 + zl, rows, 128:] = rest_of(block, 1)
            main, rest = total[:PAD], rest_of(total, 0)
            wide[:, :128] = main
            wide[:, 128:] = rest
            first = wide[:, :RANK]
            deposit(0, xh * 2 + zl, main, rest)
            second += mul(first.astype(BF16), levels[xh * 2 + zl, :, :RANK].astype(BF16))
        wide[:, :RANK] = second
        deposit(1, xh, wide[:, :128], wide[:, 128:])
    slabs[4], slabs[7] = rests
    window_ref[0] = jnp.concatenate(slabs, axis=0).astype(BF16)
    level_ref[...] = levels[own, :, :RANK].astype(BF16)
    for q in range(4):
        place = (me // 32) % 2 * 8 + (q // 2) * 4 + me // 2 % 2 * 2 + q % 2
        tail = pltpu.roll(got_ref[place].astype(F32)[2 * PAD : 2 * PAD + 24], 96, 1)
        lists_ref[q : q + 1, :] = tail[16:17].astype(I32)
        lists_ref[4 + q : 5 + q, :] = tail[17:18].astype(I32)


def couple_body(me_ref, lists_ref, up_ref, mid_ref, down_ref, own_ref, beside_ref, across_ref, opposite_ref, out_ref, rows, stack, wide):
    me = me_ref[0]
    y = me // 64
    q_own = me // 16 % 2 * 2 + me % 2
    for p, ref in enumerate((up_ref, mid_ref, down_ref)):
        for zh in range(4):
            block = ref[zh].astype(F32)
            for g in range(SLABS):
                rows[p, zh, g] = block[PAD * g : PAD * (g + 1)]
    lane = lax.broadcasted_iota(I32, (PAD, 128), 1)
    sources = ((own_ref, 0, q_own), (beside_ref, 0, q_own ^ 2), (across_ref, 432, q_own ^ 1), (opposite_ref, 0, q_own ^ 3))
    totals = [jnp.zeros((PAD, RANK), F32)] * 2
    for g in range(3):
        level = g // 2
        for which, (ref, start, q) in enumerate(sources):
            rest = jnp.zeros((PAD, 128), F32)
            for s in range(4):
                if 4 * g + s == SLOTS[0]:
                    stack[which, g, :, 128 * s : 128 * (s + 1)] = jnp.zeros((PAD, 128), BF16)
                    continue
                code = lists_ref[4 + q, s] if level else lists_ref[q, 4 * g + s]
                valid = code >= 0
                safe = jnp.where(valid, code, y * (8 if level else 16))
                row, col = (safe // 4, safe % 4) if level else (safe // 8, safe % 8)
                zh, place = (col, row % 2) if level else (col // 2, row % 2 * 2 + col % 2)
                plane = row // 2 - y + 1
                main = rows[plane, zh, 5 * level + place]
                stack[which, g, :, 128 * s : 128 * (s + 1)] = jnp.where(valid, main, 0.0).astype(BF16)
                turned = pltpu.roll(rows[plane, zh, 4 + 3 * level], (s + 4 - place) % 4 * 32, 1)
                inside = (lane >= 32 * s) & (lane < jnp.where(valid, 32 * (s + 1), 0))
                rest = jnp.where(inside, turned, rest)
            stack[which, g, :, 512:] = rest.astype(BF16)
            main = ref[start + RANK * g : start + RANK * (g + 1), :]
            last = ref[start + 3 * RANK : start + 4 * RANK, 128 * g : 128 * (g + 1)]
            totals[level] = totals[level] + mul_t(stack[which, g, :, :512], main) + mul_t(stack[which, g, :, 512:], last)
    wide[...] = jnp.zeros_like(wide)
    block = packed(totals[0], totals[1], jnp.zeros((8, 128), F32), wide)
    for d in range(8):
        out_ref[d] = block


def down_body(me_ref, got_ref, level_ref, one_ref, basis_ref, near_ref, out_ref, wide, local):
    me = me_ref[0]
    zl_own = me // 2 % 2
    for q in range(4):
        base = q // 2 * 4 + q % 2
        mine = got_ref[base + zl_own * 2].astype(F32)
        both = got_ref[base].astype(F32) + got_ref[base + 2].astype(F32)
        wide[:, :128] = both[PAD : 2 * PAD]
        wide[:, 128:] = rest_of(both, 1)
        second = wide[:, :RANK].astype(BF16)
        wide[:, :128] = mine[:PAD]
        wide[:, 128:] = rest_of(mine, 0)
        local[PAD * q : PAD * (q + 1), :] = wide[:, :RANK] + mul_t(second, level_ref[...])
    one = mul(spreader(4, 144, True), local[...].astype(BF16)).astype(BF16)
    leaf = mul_t(one, one_ref[...]).astype(BF16)
    out_ref[...] = (near_ref[...] + mul(leaf, basis_ref[...])).astype(BF16)


def slot_of(list_ref, me, apart):
    found = jnp.int32(0)
    for k in range(1, 4):
        found = jnp.where(list_ref[0, k] == me + apart, k, found)
    return found


def side_body(me_ref, list_ref, x_ref, blocks_ref, chip_ref, cross_ref, below_ref):
    me = me_ref[0]
    even = me % 2 == 0
    x = x_ref[...]
    chip_ref[0:144] = x
    cross_ref[0] = x
    right_one = mul(x, blocks_ref[slot_of(list_ref, me, 1)]).astype(BF16)
    right_two = mul(x, blocks_ref[slot_of(list_ref, me, 17)]).astype(BF16)
    left = mul(x, blocks_ref[slot_of(list_ref, me, 15)]).astype(BF16)
    below_ref[...] = mul(x, blocks_ref[slot_of(list_ref, me, 16)]).astype(BF16)

    @pl.when(even)
    def _():
        chip_ref[144:288] = right_one
        chip_ref[288:432] = right_two
        cross_ref[1] = left
        cross_ref[2] = jnp.zeros_like(left)

    @pl.when(jnp.logical_not(even))
    def _():
        cross_ref[1] = right_one
        cross_ref[2] = right_two
        chip_ref[144:288] = left
        chip_ref[288:432] = jnp.zeros_like(left)


def pack_body(one_ref, two_ref, own_ref, wide):
    wide[...] = jnp.zeros_like(wide)
    own_ref[3 * RANK :, 384:] = jnp.zeros((RANK, 128), BF16)
    for g in range(3):
        rest = jnp.zeros((RANK, 128), F32)
        for s in range(4):
            place = (slice(RANK * g, RANK * (g + 1)), slice(128 * s, 128 * (s + 1)))
            if 4 * g + s == SLOTS[0]:
                own_ref[place] = jnp.zeros((RANK, 128), BF16)
                continue
            block = one_ref[4 * g + s] if g < 2 else two_ref[s]
            own_ref[place] = block[:, :128]
            wide[:, :32] = block[:, 128:].astype(F32)
            rest += wide[...] if s == 0 else pltpu.roll(wide[...], 32 * s, 1)
        own_ref[3 * RANK :, 128 * g : 128 * (g + 1)] = rest.astype(BF16)


def turn_body(me_ref, x_ref, below_ref, chip_ref, cross_ref, rise_ref, sink_ref, mirror_ref):
    even = me_ref[0] % 2 == 0
    rise_ref[1] = x_ref[...]

    @pl.when(even)
    def _():
        rise_ref[0] = cross_ref[0]
        rise_ref[2] = chip_ref[0:144]
        mirror_ref[...] = cross_ref[1]
        sides = chip_ref[144:288].astype(F32) + cross_ref[2].astype(F32)
        sink_ref[...] = (below_ref[...].astype(F32) + sides).astype(BF16)

    @pl.when(jnp.logical_not(even))
    def _():
        rise_ref[0] = chip_ref[0:144]
        rise_ref[2] = cross_ref[0]
        mirror_ref[...] = chip_ref[144:288]
        sides = cross_ref[1].astype(F32) + chip_ref[288:432].astype(F32)
        sink_ref[...] = (below_ref[...].astype(F32) + sides).astype(BF16)


def near_body(me_ref, list_ref, self_ref, blocks_ref, rise_ref, mirror_ref, risen_ref, sunk_ref, out_ref):
    me = me_ref[0]
    total = mul_t(rise_ref[1], self_ref[...])
    total += mul_t(rise_ref[2], blocks_ref[slot_of(list_ref, me, 1)])
    total += mul_t(risen_ref[0], blocks_ref[slot_of(list_ref, me, 15)])
    total += mul_t(risen_ref[1], blocks_ref[slot_of(list_ref, me, 16)])
    total += mul_t(risen_ref[2], blocks_ref[slot_of(list_ref, me, 17)])
    out_ref[...] = total + mirror_ref[...].astype(F32) + sunk_ref[...].astype(F32)


def shards(
    right_sides,
    near_self,
    near_blocks,
    near_list,
    basis,
    transfer_one,
    transfer_two,
    couple_one,
    couple_two,
    far_list_one,
    far_list_two,
):
    me = lax.axis_index(AXES).astype(I32).reshape(1)
    x = right_sides[0, 0].T
    vectors = basis[0, 0].T
    one = transfer_one[0, 0]
    blocks = near_blocks[0, 0]
    links = near_list[0]

    across_gy = ("zh", "zl", "c")
    along_gx = ("y", "xh", "xl")
    swap = [(0, 1), (1, 0)]

    message, own, chip, cross, below = fused(
        Stage(
            up_body,
            [shape(16, ROWS, 128)],
            [pltpu.VMEM((2, PAD, 256), F32)],
            [x, vectors, one],
            direct=[transfer_two[0, 0]],
            lists=[far_list_one[0], far_list_two[0]],
            repeats={0: [d // 4 % 2 * 2 + d % 2 for d in range(16)]},
        ),
        Stage(
            pack_body,
            [shape(4 * RANK, 512)],
            [pltpu.VMEM((RANK, 128), F32)],
            [couple_one[0, 0], couple_two[0, 0]],
            also=[(0, 2, 432)],
        ),
        Stage(
            side_body,
            [shape(1072, 512), shape(3, 144, 512), shape(144, 512)],
            [],
            [x, blocks],
            lists=[links],
            scalars=[me],
            heads={0: 432},
        ),
        flops=4 * 10**8,
    )
    got = lax.all_to_all(message, ("xh", "xl", "zl", "c"), 0, 0)
    from_chip = lax.ppermute(chip, "c", swap)
    steps = [(i, i + 1) for i in range(1, 15, 2)] + [(i, i - 1) for i in range(2, 16, 2)]
    from_cross = lax.ppermute(cross, across_gy, steps)
    beside = lax.ppermute(own, "xl", swap)
    window, level, codes = fused(
        Stage(
            merge_body,
            [shape(4, SLABS * PAD, 128), shape(RANK, RANK), shape(8, 128, dtype=I32)],
            [pltpu.VMEM((PAD, 256), F32), pltpu.VMEM((4, RANK, 256), F32)],
            [got],
            scalars=[me],
            repeats={0: [0] * 4},
        ),
        flops=6 * 10**9,
    )
    plane = lax.all_to_all(window, "zh", 0, 0)
    below, _ = lax.optimization_barrier((below, window))
    rise, sink, mirror = fused(
        Stage(
            turn_body, [shape(3, 144, 512), shape(144, 512), shape(144, 512)], [], [x, below, from_chip, from_cross], scalars=[me], first_rows={2: 432}
        )
    )
    risen = lax.ppermute(rise, along_gx, [(i + 1, i) for i in range(31)])
    sunk = lax.ppermute(sink, along_gx, [(i, i + 1) for i in range(31)])
    beside, _ = lax.optimization_barrier((beside, window))
    opposite = lax.ppermute(beside, "c", swap)
    above = lax.ppermute(plane, "y", [(i, i + 1) for i in range(7)])
    under = lax.ppermute(plane, "y", [(i + 1, i) for i in range(7)])
    near = call(
        near_body, shape(144, 512, dtype=F32), [], [SMEM, SMEM] + [VMEM] * 6, 5 * 10**9, 4 * 10**6
    )(me, links, near_self[0, 0], blocks, rise, mirror, risen, sunk)
    codes = after(codes, near)
    partial = call(
        couple_body,
        shape(8, ROWS, 128),
        [
            pltpu.VMEM((3, 4, SLABS, PAD, 128), F32),
            pltpu.VMEM((4, 3, PAD, 640), BF16),
            pltpu.VMEM((2, PAD, 256), F32),
        ],
        [SMEM, SMEM] + [VMEM] * 7,
        6 * 10**8,
        4 * 10**6,
    )(me, codes, above, plane, under, own, beside, from_chip, opposite)
    sums = lax.all_to_all(partial, ("xl", "zl", "c"), 0, 0)
    applied = call(
        down_body,
        shape(144, 512),
        [pltpu.VMEM((PAD, 256), F32), pltpu.VMEM((RANK, RANK), F32)],
        [SMEM] + [VMEM] * 5,
        10**8,
        10**6,
    )(me, sums, level, one, vectors, near)
    return applied.T[None, None]


def solution(mesh):
    split = Mesh(mesh.devices.reshape(8, 2, 2, 4, 2, 2), AXES)
    rows, cols = AXES[:3], AXES[3:]

    def spec(rank):
        return P(rows, cols, *[None] * (rank - 2))

    ranks = (4, 4, 5, 3, 4, 4, 4, 5, 5, 3, 3)
    return jax.shard_map(
        shards, mesh=split, in_specs=tuple(map(spec, ranks)), out_specs=spec(4), check_vma=False
    )
```
